128 devices in a mesh: chan: 32 (over x_hi, z, y), grp: 4 (over x_lo, core).
Axes of the slice: x: 4 (x_hi: 2, x_lo: 2; x = x_hi * 2 + x_lo), y: 4, z: 4, core: 2. Of those that a mesh axis runs over, the one named last changes fastest.
Arguments:
- spectra: bfloat16 [2, 2, 1024, 1024], P(None, None, 'chan', 'grp'), may hold values from -6 to 6
- pair_channels: int32 [2, 540672], P(None, 'chan'), may hold values from 0 to 1023, as said below
- pair_counts: int32 [32], P('chan'), may hold values from 1 to 16896, as said below
Outputs:
- stacks: float32 [256, 540672], P('grp', 'chan')
The draws below stay inside these ranges and needn't reach their ends.
Inputs may be any that keep to these rules, and one draw needn't show every extreme that they name: `pair_channels`: column o * 16896 + s names owner o's pair slot s: row 0 the first channel, row 1 the second. Slots from pair_counts[o] on are unused. The live slots of one owner name distinct pairs, and at most 1024 of them have their first channel in one block of channels d * 32 to (d + 1) * 32 - 1; some owner has exactly 1024 in some block. `pair_counts`: some owner has all 16896 slots live.
All inputs are finite; a program needn't handle non-finite values.
Results may differ from the reference program's by a relative error of at most 0.0036.
Values may be sent and summed in bfloat16 or wider, within the bound.
A program may use at most 128 MiB of HBM per device.

```python
import math
import jax
import jax.numpy as jnp
from jax import lax

FREQS = 1024
LAGS = 256
WINDOWS = 2
CH_DEV = 32
CHANNELS = 1024
CAP = 1024
P_OWN = 16896
N_CHAN = 32


def pair_layout(key):
    blocks = CHANNELS // CH_DEV
    per_block = CH_DEV * CHANNELS
    keys = jax.random.split(key, 7)
    sigma = jax.random.permutation(keys[0], blocks)
    tau = jax.random.permutation(keys[1], blocks)
    profile = CAP * (jnp.arange(blocks, dtype=jnp.int32) + 1) // blocks
    level = (sigma[:, None] + tau[None, :]) % blocks
    limit = jax.random.randint(keys[2], (blocks,), 3 * CAP // 4, CAP + 1)
    chosen = jax.random.randint(keys[3], (), 0, blocks)
    limit = jnp.where(jnp.arange(blocks, dtype=jnp.int32) == chosen, CAP, limit)
    loads = jnp.minimum(profile[level], limit[None, :])
    counts = jnp.sum(loads, axis=0).astype(jnp.int32)
    run_start = jnp.cumsum(loads, axis=1) - loads
    upto = jnp.cumsum(loads, axis=0)
    offset = upto - loads
    slot = jnp.arange(P_OWN, dtype=jnp.int32)
    which = jnp.sum((upto[:, :, None] <= slot[None, None, :]).astype(jnp.int32), axis=0)
    which = jnp.minimum(which, blocks - 1)
    owners = jnp.arange(blocks, dtype=jnp.int32)[:, None]
    within = slot[None, :] - offset[which, owners]
    orders = jax.vmap(lambda sub: jax.random.permutation(sub, per_block))(jax.random.split(keys[4], blocks))
    index = jnp.clip(run_start[which, owners] + within, 0, per_block - 1)
    picked = orders[which, index]
    first = which * CH_DEV + picked // CHANNELS
    second = picked % CHANNELS
    live = slot[None, :] < counts[:, None]
    filler = jax.random.randint(keys[5], (2, blocks, P_OWN), 0, CHANNELS)
    first = jnp.where(live, first, filler[0])
    second = jnp.where(live, second, filler[1])
    score = jax.random.randint(keys[6], (blocks, P_OWN), 0, 16384) * P_OWN + slot[None, :]
    score = jnp.where(live, score, 1073741824 + slot[None, :])
    order = jnp.argsort(score, axis=1, stable=True)
    first = jnp.take_along_axis(first, order, axis=1)
    second = jnp.take_along_axis(second, order, axis=1)
    return (first.astype(jnp.int32), second.astype(jnp.int32), counts)


def draw_pair_channels(key, part):
    first, second, counts = pair_layout(key)
    return jnp.stack([first.reshape(-1), second.reshape(-1)]).astype(jnp.int32)


def draw_pair_counts(key, part):
    first, second, counts = pair_layout(key)
    return counts.astype(jnp.int32)


def level_of(stream_key, dims, cuts, smallest, largest):
    def one(dim, blocks):
        heights = jax.random.uniform(jax.random.fold_in(jax.random.fold_in(stream_key, 6), dim), (blocks,), jnp.float32, smallest / len(cuts), largest / len(cuts))
        return jnp.repeat(jnp.exp(heights), dims[dim] // blocks).reshape((-1,) + (1,) * (len(dims) - dim - 1))

    factor_of = one(*cuts[0])
    for cut in cuts[1:]:
        factor_of = factor_of * one(*cut)
    return factor_of


def normal_values(stream_key, dims, scale, reach, cuts=(), held_as=jnp.bfloat16):
    loudness = level_of(stream_key, dims, cuts, -0.22, 0.18) if cuts else 1.0
    result = jax.random.normal(stream_key, dims, jnp.float32) * scale * loudness
    return jnp.minimum(jnp.maximum(result, -reach), reach).astype(held_as)


def setup_inputs(seed: int = 0) -> dict:
    seeds = jax.random.split(jax.random.key(seed), 4)
    return {
        "spectra": normal_values(seeds[0], (2, WINDOWS, CHANNELS, FREQS), 1.0, 6.0, ((2, 32), (3, 4))),
        "pair_channels": draw_pair_channels(jax.random.fold_in(seeds[3], 71), 0),
        "pair_counts": draw_pair_counts(jax.random.fold_in(seeds[3], 71), 0),
    }


def lag_table(freq_index, lag_index, span):
    phase = jnp.mod(lag_index[:, None] * freq_index[None, :], span)
    angle = phase.astype(jnp.float32) * (2.0 * math.pi / span)
    return jnp.concatenate([jnp.cos(angle), -jnp.sin(angle)], axis=1).astype(jnp.bfloat16)

def reference(spectra, pair_channels, pair_counts):
    slots = N_CHAN * P_OWN
    width = CAP // 2
    scale = 1.0 / math.sqrt(WINDOWS * FREQS)
    freq_index = jnp.arange(FREQS, dtype=jnp.int32) + 1
    lag_index = jnp.arange(LAGS, dtype=jnp.int32) - LAGS // 2
    weights = lag_table(freq_index, lag_index, 4 * FREQS)
    first = pair_channels[0].reshape(-1, width)
    second = pair_channels[1].reshape(-1, width)

    def one_block(pair):
        left_ids, right_ids = pair
        mine = spectra[:, :, left_ids, :].astype(jnp.float32)
        other = spectra[:, :, right_ids, :].astype(jnp.float32)
        real_part = lax.optimization_barrier(jnp.sum(mine[0] * other[0] + mine[1] * other[1], axis=0))
        imag_part = lax.optimization_barrier(jnp.sum(mine[1] * other[0] - mine[0] * other[1], axis=0))
        cross = jnp.concatenate([real_part, imag_part], axis=1).astype(jnp.bfloat16)
        return lax.dot_general(weights, cross, (((1,), (1,)), ((), ())), preferred_element_type=jnp.float32)
    raw = lax.map(one_block, (first, second))
    raw = jnp.transpose(raw, (1, 0, 2)).reshape(LAGS, slots)
    live = jnp.arange(P_OWN, dtype=jnp.int32)[None, :] < pair_counts[:, None]
    live = live.reshape(slots)
    return jnp.where(live[None, :], raw * scale, 0.0)
```

```python
import functools
import math

import jax
import jax.numpy as jnp
from jax import lax
from jax.experimental import pallas as pl
from jax.experimental.pallas import tpu as pltpu
from jax.sharding import PartitionSpec as P

FREQS = 1024
LAGS = 256
WINDOWS = 2
SLOTS = 16896
NSEM = 160
VMEM = 60 << 20

AX = {"x": 0, "z": 1, "y": 2}
MESH = pl.DeviceIdType.MESH
STREAMS = [("yzx", 0, 48, 48), ("zxy", 96, 48, 32), ("xyz", 176, 32, 48)]
HALVES = {"R": "all", "L": "all", "FR": "a", "FL": "b"}
LANDS = {"R": 3, "L": 1, "FR": 2, "FL": 2}

def where():
    chan, grp = lax.axis_index("chan"), lax.axis_index("grp")
    return [2 * (chan // 16) + grp // 2, (chan // 4) % 4, chan % 4], grp % 2

def device(pos, core):
    x, z, y = pos
    return ((x // 2) * 16 + z * 4 + y, (x % 2) * 2 + core)

def moved(pos, axis, by):
    new = list(pos); new[AX[axis]] = (pos[AX[axis]] + by + 4) % 4
    return new

class Gather:
    def __init__(self, buf, send_sems, recv_sems):
        self.buf, self.ss, self.rs = buf, send_sems, recv_sems
        self.pos, self.core = where()
        self.twin = device(self.pos, 1 - self.core)
        self.n = 0
        self.sent, self.shared, self.ids = [], [], {}
    def enter(self):
        bar = pltpu.get_barrier_semaphore()
        for ax in "xzy":
            for by in (1, -1):
                pl.semaphore_signal(bar, inc=1, device_id=device(moved(self.pos, ax, by), self.core), device_id_type=MESH)
        pl.semaphore_signal(bar, inc=1, device_id=self.twin, device_id_type=MESH)
        pl.semaphore_wait(bar, 7)
    def view(self, s, sel, part="all", core=0):
        order, r0, ha, hb = STREAMS[s]
        rows = {"all": (r0, ha + hb), "a": (r0, ha), "b": (r0 + ha, hb)}[part]
        ix = [0, 0, 0]
        for ax, v in zip(order, sel):
            ix[AX[ax]] = v
        return self.buf.at[(core, *ix, pl.ds(*rows))]
    def copy(self, src, dst, k, to):
        return pltpu.make_async_remote_copy(src_ref=src, dst_ref=dst, send_sem=self.ss.at[k], recv_sem=self.rs.at[k], device_id=to, device_id_type=MESH)
    def go(self, src, dst, to):
        k = self.n; self.n += 1
        c = self.copy(src, dst, k, to); c.start(); self.sent.append(c)
        return k
    def sel(self, phase, chunk, rel):
        return (*chunk[:phase], rel)
    def send(self, s, phase, chunk, kind):
        ax = STREAMS[s][0][phase]
        by = 1 if kind in ("R", "FR") else -1
        src_rel = {"R": 0, "L": 0, "FR": 3, "FL": 1}[kind]
        part = HALVES[kind]
        k = self.go(self.view(s, (*chunk, src_rel), part), self.view(s, (*chunk, LANDS[kind]), part), device(moved(self.pos, ax, by), self.core))
        self.ids[s, phase, str(chunk), kind] = k
    def both(self, s, phase, chunk):
        self.send(s, phase, chunk, "R"); self.send(s, phase, chunk, "L")
    def wait(self, s, phase, chunk, kind):
        ref = self.view(s, (*chunk, LANDS[kind]), HALVES[kind])
        self.copy(ref, ref, self.ids[s, phase, str(chunk), kind], self.twin).wait_recv()
    def pass_on(self, s, phase, chunk, kind):
        self.wait(s, phase, chunk, kind)
        self.send(s, phase, chunk, "F" + kind)
    def share(self, s, sel, part="all"):
        k = self.go(self.view(s, sel, part, 0), self.view(s, sel, part, 1), self.twin)
        self.shared.append((k, s, sel, part))

ALL, REST = slice(0, 4), slice(1, 4)

def run_gather(x_ref, buf, ss, rs):
    g = Gather(buf, ss, rs)
    S = range(len(STREAMS))
    buf[0, 0, 0, 0] = x_ref[...]
    g.enter()
    for s in S: g.both(s, 0, ())
    for s in S: g.both(s, 1, (0,))
    for s in S: g.both(s, 2, (0, 0))
    for s in S:
        g.pass_on(s, 0, (), "R"); g.pass_on(s, 0, (), "L")
    for s in S:
        g.pass_on(s, 1, (0,), "R"); g.pass_on(s, 1, (0,), "L")
    for s in S:
        g.wait(s, 0, (), "FR"); g.wait(s, 0, (), "FL")
        g.both(s, 1, (REST,));
    for s in S:
        g.both(s, 2, (REST, 0))
    for s in S:
        g.pass_on(s, 2, (0, 0), "R"); g.pass_on(s, 2, (0, 0), "L")
    for s in S:
        g.wait(s, 1, (0,), "FR"); g.wait(s, 1, (0,), "FL")
    for s in S:
        g.pass_on(s, 1, (REST,), "R")
        g.both(s, 2, (ALL, 3))
        g.pass_on(s, 1, (REST,), "L")
        g.both(s, 2, (ALL, 1))
    for s in S:
        g.pass_on(s, 2, (REST, 0), "R"); g.pass_on(s, 2, (REST, 0), "L")
        g.share(s, (ALL, 0, 3)); g.share(s, (ALL, 0, 1))
    for s in S:
        g.wait(s, 1, (REST,), "FR"); g.wait(s, 1, (REST,), "FL")
        g.both(s, 2, (ALL, 2))
        g.share(s, (ALL, ALL, 0))
    for s in S:
        g.wait(s, 2, (0, 0), "FR"); g.wait(s, 2, (0, 0), "FL")
    for b in (3, 1):
        for s in S:
            g.pass_on(s, 2, (ALL, b), "R"); g.share(s, (ALL, b, 3))
            g.pass_on(s, 2, (ALL, b), "L"); g.share(s, (ALL, b, 1))
    for s in S:
        g.wait(s, 2, (REST, 0), "FR"); g.share(s, (ALL, 0, 2), "a")
        g.wait(s, 2, (REST, 0), "FL"); g.share(s, (ALL, 0, 2), "b")
    for s in S:
        g.pass_on(s, 2, (ALL, 2), "R"); g.share(s, (ALL, 2, 3))
        g.pass_on(s, 2, (ALL, 2), "L"); g.share(s, (ALL, 2, 1))
    for b in (3, 1, 2):
        for s in S:
            g.wait(s, 2, (ALL, b), "FR"); g.share(s, (ALL, b, 2), "a")
            g.wait(s, 2, (ALL, b), "FL"); g.share(s, (ALL, b, 2), "b")
    for k, s, sel, part in g.shared:
        ref = g.view(s, sel, part, 1)
        g.copy(ref, ref, k, g.twin).wait_recv()
    for c in g.sent:
        c.wait_send()
    return g.n


def gather_kernel(x_ref, o_ref, ss, rs):
    run_gather(x_ref, o_ref, ss, rs)


def gather(x):
    return pl.pallas_call(
        gather_kernel,
        out_shape=jax.ShapeDtypeStruct((2, 4, 4, 4, 256, 128), jnp.bfloat16),
        in_specs=[pl.BlockSpec(memory_space=pltpu.VMEM)],
        out_specs=pl.BlockSpec(memory_space=pltpu.VMEM),
        scratch_shapes=[pltpu.SemaphoreType.DMA((NSEM,)), pltpu.SemaphoreType.DMA((NSEM,))],
        compiler_params=pltpu.CompilerParams(collective_id=0, has_side_effects=True, vmem_limit_bytes=VMEM),
    )(x)


def prep(s):
    w = lax.all_gather(s, "grp", axis=3, tiled=True)
    w = lax.dynamic_slice_in_dim(w, lax.axis_index("grp") * 8, 8, axis=2)
    return w.transpose(2, 0, 1, 3).reshape(256, 128)


BLOCK = 384
HALF = SLOTS // 2
UNROLL = 32
STRIDE = BLOCK + 8


def local_kernel(a_ref, b_ref, misc_ref, g_ref, w_ref, own_ref, other_ref, f_ref, x_ref):
    step = pl.program_id(0)

    @pl.when(step == 0)
    def _():
        def widen(i, c):
            rows = pl.ds(pl.multiple_of(i * 256, 256), 256)
            f_ref[rows, :] = g_ref[rows, :].astype(jnp.float32)
            return c

        lax.fori_loop(0, 128, widen, 0)

    base = step * BLOCK

    def rows_of(at):
        at = pl.multiple_of(at, 32)
        return [f_ref[pl.ds(at + 8 * i, 8), :] for i in range(4)]

    def body(i, c):
        loaded = []
        for u in range(UNROLL):
            p = i * UNROLL + u
            loaded.append((rows_of(a_ref[base + p]), rows_of(b_ref[base + p])))
        for u in range(UNROLL):
            p = i * UNROLL + u
            (ar0, ar1, ai0, ai1), (br0, br1, bi0, bi1) = loaded[u]
            re = (ar0 * br0 + ai0 * bi0) + (ar1 * br1 + ai1 * bi1)
            im = (ai0 * br0 - ar0 * bi0) + (ai1 * br1 - ar1 * bi1)
            x_ref[pl.ds(p, 8, stride=STRIDE), :] = re
            x_ref[pl.ds(p + 8 * STRIDE, 8, stride=STRIDE), :] = im
        return c

    lax.fori_loop(0, BLOCK // UNROLL, body, 0)
    parts = [x_ref[j * STRIDE:j * STRIDE + BLOCK, :] for j in range(16)]
    xb = jnp.concatenate(parts, axis=1).astype(jnp.bfloat16)
    raw = lax.dot_general(w_ref[...], xb, (((1,), (1,)), ((), ())), preferred_element_type=jnp.float32)
    slot = misc_ref[1] * HALF + base + lax.broadcasted_iota(jnp.int32, (128, BLOCK), 1)
    raw = jnp.where(slot < misc_ref[0], raw * (1.0 / math.sqrt(WINDOWS * FREQS)), 0.0)
    own_ref[...] = raw[:64]
    other_ref[...] = raw[64:].astype(other_ref.dtype)


def local(a, b, misc, g, w):
    smem = pl.BlockSpec(memory_space=pltpu.SMEM)
    steps = HALF // BLOCK
    return pl.pallas_call(
        local_kernel,
        grid_spec=pltpu.PrefetchScalarGridSpec(
            num_scalar_prefetch=3,
            grid=(steps,),
            in_specs=[
                pl.BlockSpec((32768, 128), lambda i, a, b, m: (0, 0), pipeline_mode=pl.Buffered(1)),
                pl.BlockSpec((128, 2048), lambda i, a, b, m: (0, 0)),
            ],
            out_specs=[
                pl.BlockSpec((64, BLOCK), lambda i, a, b, m: (0, m[1] * steps + i)),
                pl.BlockSpec((64, BLOCK), lambda i, a, b, m: (0, i)),
            ],
            scratch_shapes=[
                pltpu.VMEM((32768, 128), jnp.float32),
                pltpu.VMEM((16 * STRIDE, 128), jnp.float32),
            ],
        ),
        out_shape=[
            jax.ShapeDtypeStruct((64, SLOTS), jnp.float32),
            jax.ShapeDtypeStruct((64, HALF), jnp.bfloat16),
        ],
        compiler_params=pltpu.CompilerParams(vmem_limit_bytes=VMEM),
    )(a, b, misc, g, w)


def fill_kernel(m_ref, got_ref, full_ref, o_ref):
    o_ref[...] = got_ref[...].astype(jnp.float32)


def fill(misc, got, full):
    return pl.pallas_call(
        fill_kernel,
        grid_spec=pltpu.PrefetchScalarGridSpec(
            num_scalar_prefetch=1,
            grid=(3,),
            in_specs=[
                pl.BlockSpec((64, HALF // 3), lambda i, m: (0, i)),
                pl.BlockSpec(memory_space=pl.ANY),
            ],
            out_specs=pl.BlockSpec((64, HALF // 3), lambda i, m: (0, (1 - m[1]) * 3 + i)),
        ),
        out_shape=jax.ShapeDtypeStruct((64, SLOTS), jnp.float32),
        input_output_aliases={2: 0},
        compiler_params=pltpu.CompilerParams(vmem_limit_bytes=VMEM),
    )(misc, got, full)


def lag_table(freq_index, lag_index, span):
    phase = jnp.mod(lag_index[:, None] * freq_index[None, :], span)
    angle = phase.astype(jnp.float32) * (2.0 * math.pi / span)
    return jnp.concatenate([jnp.cos(angle), -jnp.sin(angle)], axis=1).astype(jnp.bfloat16)


def place_of(channel):
    (x0, z0, y0), core0 = where()
    xh, z, y = channel >> 9, (channel >> 7) & 3, (channel >> 5) & 3
    xl, core = (channel >> 4) & 1, (channel >> 3) & 1
    rx, rz, ry = (2 * xh + xl - x0) & 3, (z - z0) & 3, (y - y0) & 3
    pos = ((((core ^ core0) * 4 + rx) * 4 + rz) * 4 + ry)
    return pos * 256 + (channel & 7) * 32


def on_device(spectra, pair_channels, pair_counts):
    grp = lax.axis_index("grp")
    core = grp % 2
    mine = lax.dynamic_slice_in_dim(pair_channels, core * HALF, HALF, axis=1)
    rows = place_of(mine)
    short = LAGS // 4
    lags = jnp.arange(short, dtype=jnp.int32) - LAGS // 2
    lag_index = jnp.concatenate([lags + grp * short, lags + (grp ^ 1) * short])
    freq_index = jnp.arange(FREQS, dtype=jnp.int32) + 1
    weights = lag_table(freq_index, lag_index, 4 * FREQS)
    misc = jnp.stack([pair_counts[0], core.astype(jnp.int32)])
    full = gather(prep(spectra)).reshape(32768, 128)
    own, other = local(rows[0], rows[1], misc, full, weights)
    got = lax.ppermute(other, "grp", [(i, i ^ 1) for i in range(4)])
    return fill(misc, got, own)


def solution(mesh):
    placed = (P(None, None, "chan", "grp"), P(None, "chan"), P("chan"))
    return jax.shard_map(
        on_device, mesh=mesh, in_specs=placed, out_specs=P("grp", "chan"), check_vma=False
    )
```

```python
import functools
import math

import jax
import jax.numpy as jnp
import ml_dtypes
import numpy as np
from jax import lax
from jax.experimental import pallas as pl
from jax.experimental.pallas import tpu as pltpu
from jax.sharding import PartitionSpec as P

FREQS = 1024
LAGS = 256
WINDOWS = 2
SLOTS = 16896
NSEM = 192
VMEM = 60 << 20
SHORT = LAGS // 4

BLOCK = 384
BOTH = 9
ALONE = 4
assert 4 * BOTH + 2 * ALONE == SLOTS // BLOCK
MINE = (BOTH + ALONE) * BLOCK
UNROLL = 32
STRIDE = BLOCK + 8

AX = {"x": 0, "z": 1, "y": 2}
MESH = pl.DeviceIdType.MESH
STREAMS = [("yzx", 0, 3, 3), ("zxy", 6, 3, 2), ("xyz", 11, 2, 3)]
HALVES = {"R": "all", "L": "all", "FR": "a", "FL": "b"}
LANDS = {"R": 3, "L": 1, "FR": 2, "FL": 2}

def where():
    chan, grp = lax.axis_index("chan"), lax.axis_index("grp")
    return [2 * (chan // 16) + grp // 2, (chan // 4) % 4, chan % 4], grp % 2

def device(pos, core):
    x, z, y = pos
    return ((x // 2) * 16 + z * 4 + y, (x % 2) * 2 + core)

def moved(pos, axis, by):
    new = list(pos); new[AX[axis]] = (pos[AX[axis]] + by + 4) % 4
    return new

class Gather:
    def __init__(self, buf, send_sems, recv_sems):
        self.buf, self.ss, self.rs = buf, send_sems, recv_sems
        self.pos, self.core = where()
        self.twin = device(self.pos, 1 - self.core)
        peer = [self.pos[0] ^ 1, self.pos[1], self.pos[2]]
        self.group = [None, self.twin, device(peer, self.core), device(peer, 1 - self.core)]
        self.n = 0
        self.sent, self.shared, self.ids = [], [], {}
    def enter(self):
        bar = pltpu.get_barrier_semaphore()
        for ax in "xzy":
            for by in (1, -1):
                pl.semaphore_signal(bar, inc=1, device_id=device(moved(self.pos, ax, by), self.core), device_id_type=MESH)
        for to in (self.twin, self.group[3]):
            pl.semaphore_signal(bar, inc=1, device_id=to, device_id_type=MESH)
        pl.semaphore_wait(bar, 8)
    def view(self, s, sel, part="all", core=0):
        order, r0, ha, hb = STREAMS[s]
        rows = {"all": (r0, ha + hb), "a": (r0, ha), "b": (r0 + ha, hb)}[part]
        ix = [0, 0, 0]
        for ax, v in zip(order, sel):
            ix[AX[ax]] = v
        return self.buf.at[(core, *ix, pl.ds(*rows))]
    def copy(self, src, dst, k, to):
        return pltpu.make_async_remote_copy(src_ref=src, dst_ref=dst, send_sem=self.ss.at[k], recv_sem=self.rs.at[k], device_id=to, device_id_type=MESH)
    def go(self, src, dst, to):
        k = self.n; self.n += 1
        c = self.copy(src, dst, k, to); c.start(); self.sent.append(c)
        return k
    def sel(self, phase, chunk, rel):
        return (*chunk[:phase], rel)
    def send(self, s, phase, chunk, kind):
        ax = STREAMS[s][0][phase]
        by = 1 if kind in ("R", "FR") else -1
        src_rel = {"R": 0, "L": 0, "FR": 3, "FL": 1}[kind]
        part = HALVES[kind]
        k = self.go(self.view(s, (*chunk, src_rel), part), self.view(s, (*chunk, LANDS[kind]), part), device(moved(self.pos, ax, by), self.core))
        self.ids[s, phase, str(chunk), kind] = k
    def both(self, s, phase, chunk):
        self.send(s, phase, chunk, "R"); self.send(s, phase, chunk, "L")
    def wait(self, s, phase, chunk, kind):
        ref = self.view(s, (*chunk, LANDS[kind]), HALVES[kind])
        self.copy(ref, ref, self.ids[s, phase, str(chunk), kind], self.twin).wait_recv()
    def pass_on(self, s, phase, chunk, kind):
        self.wait(s, phase, chunk, kind)
        self.send(s, phase, chunk, "F" + kind)
    def share(self, s, sel, part="all"):
        k = self.go(self.view(s, sel, part, 0), self.view(s, sel, part, 1), self.twin)
        self.shared.append((k, s, sel, part))

ALL, REST = slice(0, 4), slice(1, 4)

def regroup(g, x_ref, part_ref, wide_ref, mixed_ref):
    grp = lax.axis_index("grp")
    ks = [g.go(x_ref.at[grp ^ k], part_ref.at[k], g.group[k]) for k in (1, 2, 3)]
    for k in range(4):
        if k:
            g.copy(part_ref.at[k], part_ref.at[k], ks[k - 1], g.twin).wait_recv()
            got = part_ref[k]
        else:
            got = x_ref[grp]
        wide_ref[...] = got.astype(jnp.float32)
        for r in range(2):
            for q in range(0, 32, 8):
                mixed_ref[pl.ds(8 * q + 2 * (grp ^ k) + r, 8, stride=8), :] = wide_ref[pl.ds(2 * q + r, 8, stride=2), :]
    g.buf[0, 0, 0, 0] = mixed_ref[...].astype(jnp.bfloat16).reshape(16, 16, 128)


def run_gather(g):
    S = range(len(STREAMS))
    for s in S: g.both(s, 0, ())
    for s in S: g.both(s, 1, (0,))
    for s in S: g.both(s, 2, (0, 0))
    for s in S:
        g.pass_on(s, 0, (), "R"); g.pass_on(s, 0, (), "L")
    for s in S:
        g.pass_on(s, 1, (0,), "R"); g.pass_on(s, 1, (0,), "L")
    for s in S:
        g.wait(s, 0, (), "FR"); g.wait(s, 0, (), "FL")
        g.both(s, 1, (REST,));
    for s in S:
        g.both(s, 2, (REST, 0))
    for s in S:
        g.pass_on(s, 2, (0, 0), "R"); g.pass_on(s, 2, (0, 0), "L")
    for s in S:
        g.wait(s, 1, (0,), "FR"); g.wait(s, 1, (0,), "FL")
    for s in S:
        g.pass_on(s, 1, (REST,), "R")
        g.both(s, 2, (ALL, 3))
        g.pass_on(s, 1, (REST,), "L")
        g.both(s, 2, (ALL, 1))
    for s in S:
        g.pass_on(s, 2, (REST, 0), "R"); g.pass_on(s, 2, (REST, 0), "L")
        g.share(s, (ALL, 0, 3)); g.share(s, (ALL, 0, 1))
    for s in S:
        g.wait(s, 1, (REST,), "FR"); g.wait(s, 1, (REST,), "FL")
        g.both(s, 2, (ALL, 2))
        g.share(s, (ALL, ALL, 0))
    for s in S:
        g.wait(s, 2, (0, 0), "FR"); g.wait(s, 2, (0, 0), "FL")
    for b in (3, 1):
        for s in S:
            g.pass_on(s, 2, (ALL, b), "R"); g.share(s, (ALL, b, 3))
            g.pass_on(s, 2, (ALL, b), "L"); g.share(s, (ALL, b, 1))
    for s in S:
        g.wait(s, 2, (REST, 0), "FR"); g.share(s, (ALL, 0, 2), "a")
        g.wait(s, 2, (REST, 0), "FL"); g.share(s, (ALL, 0, 2), "b")
    for s in S:
        g.pass_on(s, 2, (ALL, 2), "R"); g.share(s, (ALL, 2, 3))
        g.pass_on(s, 2, (ALL, 2), "L"); g.share(s, (ALL, 2, 1))
    for b in (3, 1, 2):
        for s in S:
            g.wait(s, 2, (ALL, b), "FR"); g.share(s, (ALL, b, 2), "a")
            g.wait(s, 2, (ALL, b), "FL"); g.share(s, (ALL, b, 2), "b")
    for k, s, sel, part in g.shared:
        ref = g.view(s, sel, part, 1)
        g.copy(ref, ref, k, g.twin).wait_recv()


def kernel(a_ref, b_ref, x_ref, w_ref, o_ref, buf, part_ref, wide_ref, mixed_ref, prod_ref, made_ref, ss, rs):
    g = Gather(buf, ss, rs)
    g.enter()
    regroup(g, x_ref, part_ref, wide_ref, mixed_ref)
    run_gather(g)
    grp = lax.axis_index("grp")
    core = grp % 2
    rows = buf.reshape(2048, 16, 128)
    first = g.n

    def products(base):
        def body(i, c):
            loaded = []
            for u in range(UNROLL):
                p = base + i * UNROLL + u
                a, b = a_ref[p], b_ref[p]
                loaded.append((rows[a], rows[a + 1], rows[b], rows[b + 1]))
            for u in range(UNROLL):
                p = i * UNROLL + u
                ar, ai, br, bi = [v.astype(jnp.float32) for v in loaded[u]]
                re = ar * br + ai * bi
                im = ai * br - ar * bi
                prod_ref[pl.ds(p, 8, stride=STRIDE), :] = re[:8] + re[8:]
                prod_ref[pl.ds(p + 8 * STRIDE, 8, stride=STRIDE), :] = im[:8] + im[8:]
            return c

        lax.fori_loop(0, BLOCK // UNROLL, body, 0)

    def lagged(w):
        cross = jnp.concatenate([prod_ref[j * STRIDE:j * STRIDE + BLOCK, :] for j in range(16)], axis=1)
        return lax.dot_general(
            w, cross.astype(jnp.bfloat16), (((1,), (1,)), ((), ())), preferred_element_type=jnp.float32
        ).astype(jnp.bfloat16)

    def columns(block):
        return pl.ds(pl.multiple_of(block * BLOCK, 128), BLOCK)

    def lags_of(group):
        return pl.ds(pl.multiple_of(group * SHORT, SHORT), SHORT)

    def result(j, k, block, sem):
        return pltpu.make_async_remote_copy(
            src_ref=made_ref.at[j, lags_of(grp ^ k)], dst_ref=o_ref.at[:, columns(block)],
            send_sem=ss.at[sem], recv_sem=rs.at[sem], device_id=g.group[k], device_id_type=MESH)

    def both(j, c):
        products(j * BLOCK)
        made_ref[j] = lagged(w_ref[...])
        block = grp * BOTH + j
        o_ref[:, columns(block)] = made_ref[j, lags_of(grp), :]
        for k in (2, 3, 1):
            result(j, k, block, first + 3 * j + k - 1).start()
        return c

    def alone(j, c):
        products((BOTH + j) * BLOCK)
        chip = pl.ds(pl.multiple_of(grp // 2 * 128, 128), 128)
        made_ref[BOTH + j, chip, :] = lagged(w_ref[chip, :])
        block = 4 * BOTH + core * ALONE + j
        o_ref[:, columns(block)] = made_ref[BOTH + j, lags_of(grp), :]
        result(BOTH + j, 1, block, first + 3 * BOTH + j).start()
        return c

    lax.fori_loop(0, BOTH, both, 0)
    lax.fori_loop(0, ALONE, alone, 0)

    def end_both(j, c):
        for k in (1, 2, 3):
            sem = first + 3 * j + k - 1
            result(j, k, grp * BOTH + j, sem).wait_send()
            result(j, k, (grp ^ k) * BOTH + j, sem).wait_recv()
        return c

    def end_alone(j, c):
        sem = first + 3 * BOTH + j
        result(BOTH + j, 1, 4 * BOTH + core * ALONE + j, sem).wait_send()
        result(BOTH + j, 1, 4 * BOTH + (1 - core) * ALONE + j, sem).wait_recv()
        return c

    lax.fori_loop(0, BOTH, end_both, 0)
    lax.fori_loop(0, ALONE, end_alone, 0)
    for c in g.sent:
        c.wait_send()
    assert first + 3 * BOTH + ALONE <= NSEM


def stack(a, b, x, w):
    smem, vmem = pl.BlockSpec(memory_space=pltpu.SMEM), pl.BlockSpec(memory_space=pltpu.VMEM)
    return pl.pallas_call(
        kernel,
        out_shape=jax.ShapeDtypeStruct((SHORT, SLOTS), jnp.bfloat16),
        in_specs=[smem, smem, vmem, vmem],
        out_specs=vmem,
        scratch_shapes=[
            pltpu.VMEM((2, 4, 4, 4, 16, 16, 128), jnp.bfloat16),
            pltpu.VMEM((4, 64, 128), jnp.bfloat16),
            pltpu.VMEM((64, 128), jnp.float32),
            pltpu.VMEM((256, 128), jnp.float32),
            pltpu.VMEM((16 * STRIDE, 128), jnp.float32),
            pltpu.VMEM((BOTH + ALONE, LAGS, BLOCK), jnp.bfloat16),
            pltpu.SemaphoreType.DMA((NSEM,)),
            pltpu.SemaphoreType.DMA((NSEM,)),
        ],
        compiler_params=pltpu.CompilerParams(collective_id=0, has_side_effects=True, vmem_limit_bytes=VMEM),
    )(a, b, x, w)


def lag_table():
    span = 4 * FREQS
    lag_index = np.arange(LAGS, dtype=np.int32) - LAGS // 2
    freq_index = np.arange(FREQS, dtype=np.int32) + 1
    phase = np.mod(lag_index[:, None] * freq_index[None, :], span)
    angle = phase.astype(np.float32) * np.float32(2.0 * math.pi / span)
    return np.concatenate([np.cos(angle), -np.sin(angle)], axis=1).astype(ml_dtypes.bfloat16)


def place_of(channel):
    (x0, z0, y0), core0 = where()
    xh, z, y = channel >> 9, (channel >> 7) & 3, (channel >> 5) & 3
    xl, core = (channel >> 4) & 1, (channel >> 3) & 1
    rx, rz, ry = (2 * xh + xl - x0) & 3, (z - z0) & 3, (y - y0) & 3
    pos = ((((core ^ core0) * 4 + rx) * 4 + rz) * 4 + ry)
    return pos * 16 + (channel & 7) * 2


def on_device(spectra, pair_channels, pair_counts):
    grp = lax.axis_index("grp")
    shared = lax.dynamic_slice_in_dim(pair_channels, grp * (BOTH * BLOCK), BOTH * BLOCK, axis=1)
    alone = lax.dynamic_slice_in_dim(pair_channels, (4 * BOTH + grp % 2 * ALONE) * BLOCK, ALONE * BLOCK, axis=1)
    rows = place_of(jnp.concatenate([shared, alone], axis=1))
    x = spectra.transpose(2, 0, 1, 3).reshape(4, 64, 128)
    raw = stack(rows[0], rows[1], x, jnp.asarray(lag_table()))
    live = jnp.arange(SLOTS, dtype=jnp.int32)[None, :] < pair_counts[0]
    return jnp.where(live, raw.astype(jnp.float32) * (1.0 / math.sqrt(WINDOWS * FREQS)), 0.0)


def solution(mesh):
    placed = (P(None, None, "chan", "grp"), P(None, "chan"), P("chan"))
    return jax.shard_map(
        on_device, mesh=mesh, in_specs=placed, out_specs=P("grp", "chan"), check_vma=False
    )
```

```python
import functools
import math

import jax
import jax.numpy as jnp
import ml_dtypes
import numpy as np
from jax import lax
from jax.experimental import pallas as pl
from jax.experimental.pallas import tpu as pltpu
from jax.sharding import PartitionSpec as P

FREQS = 1024
LAGS = 256
WINDOWS = 2
SLOTS = 16896
NSEM = 126
SENDS = 24
VMEM = 60 << 20
SHORT = LAGS // 4

BLOCK = 384
BOTH = 9
ALONE = 4
assert 4 * BOTH + 2 * ALONE == SLOTS // BLOCK
MINE = (BOTH + ALONE) * BLOCK
UNROLL = 32
STRIDE = BLOCK + 8
BEHIND = 6

AX = {"x": 0, "z": 1, "y": 2}
MESH = pl.DeviceIdType.MESH
STREAMS = [("yzx", 0, 3, 3), ("zxy", 6, 3, 2), ("xyz", 11, 2, 3)]
HALVES = {"R": "all", "L": "all", "O": "all", "FR": "a", "FL": "b"}
LANDS = {"R": 3, "L": 1, "O": 2, "FR": 2, "FL": 2}

def where():
    chan, grp = lax.axis_index("chan"), lax.axis_index("grp")
    return [2 * (chan // 16) + grp // 2, (chan // 4) % 4, chan % 4], grp % 2

def device(pos, core):
    x, z, y = pos
    return ((x // 2) * 16 + z * 4 + y, (x % 2) * 2 + core)

def moved(pos, axis, by):
    new = list(pos); new[AX[axis]] = (pos[AX[axis]] + by + 4) % 4
    return new

class Gather:
    def __init__(self, buf, table, send_sems, recv_sems):
        self.table = table
        self.buf, self.ss, self.rs = buf, send_sems, recv_sems
        self.pos, self.core = where()
        self.twin = device(self.pos, 1 - self.core)
        peer = [self.pos[0] ^ 1, self.pos[1], self.pos[2]]
        self.group = [None, self.twin, device(peer, self.core), device(peer, 1 - self.core)]
        self.n = 0
        self.sent, self.shared, self.ids = [], [], {}
    def knock(self):
        bar = pltpu.get_barrier_semaphore()
        for ax in "xzy":
            for by in (1, 2, -1):
                pl.semaphore_signal(bar, inc=1, device_id=device(moved(self.pos, ax, by), self.core), device_id_type=MESH)
        for to in (self.twin, self.group[3]):
            pl.semaphore_signal(bar, inc=1, device_id=to, device_id_type=MESH)

    def enter(self):
        pl.semaphore_wait(pltpu.get_barrier_semaphore(), 11)
    def view(self, s, sel, part="all", core=0):
        order, r0, ha, hb = STREAMS[s]
        rows = {"all": (r0, ha + hb), "a": (r0, ha), "b": (r0 + ha, hb)}[part]
        ix = [0, 0, 0]
        for ax, v in zip(order, sel):
            ix[AX[ax]] = v
        return self.buf.at[(core, *ix, pl.ds(*rows))]
    def copy(self, src, dst, k, to):
        return pltpu.make_async_remote_copy(src_ref=src, dst_ref=dst, send_sem=self.ss.at[k % SENDS], recv_sem=self.rs.at[k], device_id=to, device_id_type=MESH)
    def go(self, src, dst, to):
        k = self.n; self.n += 1
        if len(self.sent) == SENDS:
            self.sent.pop(0).wait_send()
        c = self.copy(src, dst, k, to); c.start(); self.sent.append(c)
        return k
    def sel(self, phase, chunk, rel):
        return (*chunk[:phase], rel)
    def send(self, s, phase, chunk, kind):
        ax = STREAMS[s][0][phase]
        by = {"R": 1, "FR": 1, "L": -1, "FL": -1, "O": 2}[kind]
        src_rel = {"R": 0, "L": 0, "O": 0, "FR": 3, "FL": 1}[kind]
        part = HALVES[kind]
        k = self.go(self.view(s, (*chunk, src_rel), part), self.view(s, (*chunk, LANDS[kind]), part), device(moved(self.pos, ax, by), self.core))
        self.ids[s, phase, str(chunk), kind] = k
    def both(self, s, phase, chunk):
        self.send(s, phase, chunk, "R"); self.send(s, phase, chunk, "L")
    def three(self, s, phase, chunk):
        self.both(s, phase, chunk); self.send(s, phase, chunk, "O")
    def wait3(self, s, phase, chunk):
        for kind in ("R", "L", "O"):
            self.wait(s, phase, chunk, kind)
    def wait(self, s, phase, chunk, kind):
        ref = self.view(s, (*chunk, LANDS[kind]), HALVES[kind])
        self.copy(ref, ref, self.ids[s, phase, str(chunk), kind], self.twin).wait_recv()
    def pass_on(self, s, phase, chunk, kind):
        self.wait(s, phase, chunk, kind)
        self.send(s, phase, chunk, "F" + kind)
    def share(self, s, sel, part="all"):
        k = self.go(self.view(s, sel, part, 0), self.view(s, sel, part, 1), self.twin)
        self.shared.append((k, s, sel, part))
        if len(self.shared) > BEHIND:
            self.widen(*self.shared.pop(0))

    def widen(self, k, s, sel, part):
        ref = self.view(s, sel, part, 1)
        self.copy(ref, ref, k, self.twin).wait_recv()
        order, u0, ha, hb = STREAMS[s]
        units = {"all": (u0, ha + hb), "a": (u0, ha), "b": (u0 + ha, hb)}[part]
        spans = [(v.start, v.stop - v.start) if isinstance(v, slice) else (v, 1) for v in sel]

        def one(i, c):
            ix = [0, 0, 0]
            for ax, (first, n) in zip(reversed(order), reversed(spans)):
                ix[AX[ax]] = first + i % n
                i = i // n
            for core in (0, 1):
                at = (core, *ix, pl.ds(*units))
                self.table[at] = self.buf[at].astype(jnp.float32).reshape(units[1], 2, 8, 128)
            return c

        lax.fori_loop(0, math.prod(n for _, n in spans), one, 0)


ALL, REST = slice(0, 4), slice(1, 4)

def regroup(g, wide_ref, part_ref, mixed_ref):
    grp = lax.axis_index("grp")

    def rows_for(group):
        return wide_ref.at[:, pl.ds(pl.multiple_of(8 * group, 8), 8), :]

    ks = [g.go(rows_for(grp ^ k), part_ref.at[k], g.group[k]) for k in (1, 2, 3)]
    for k in range(4):
        got = part_ref.at[k] if k else rows_for(grp)
        if k:
            g.copy(got, got, ks[k - 1], g.twin).wait_recv()
        for plane in range(4):
            for r in range(2):
                mixed_ref[pl.ds(8 * plane + 2 * (grp ^ k) + r, 8, stride=32), :] = got[plane, :, r * 128:(r + 1) * 128]
    g.buf[0, 0, 0, 0] = mixed_ref[...].astype(jnp.bfloat16).reshape(16, 16, 128)


def run_gather(g):
    S = range(len(STREAMS))
    for s in S: g.three(s, 0, ())
    for s in S: g.three(s, 1, (0,))
    for s in S: g.both(s, 2, (0, 0))
    for s in S:
        g.wait3(s, 0, ())
        g.three(s, 1, (REST,))
    for s in S:
        g.both(s, 2, (REST, 0))
    for s in S:
        g.pass_on(s, 2, (0, 0), "R"); g.pass_on(s, 2, (0, 0), "L")
    for s in S:
        g.wait3(s, 1, (0,))
    for s in S:
        g.wait(s, 1, (REST,), "R")
        g.both(s, 2, (ALL, 3))
        g.wait(s, 1, (REST,), "L")
        g.both(s, 2, (ALL, 1))
    for s in S:
        g.pass_on(s, 2, (REST, 0), "R"); g.pass_on(s, 2, (REST, 0), "L")
        g.share(s, (ALL, 0, 3)); g.share(s, (ALL, 0, 1))
    for s in S:
        g.wait(s, 1, (REST,), "O")
        g.three(s, 2, (ALL, 2))
        g.share(s, (ALL, ALL, 0))
    for s in S:
        g.wait(s, 2, (0, 0), "FR"); g.wait(s, 2, (0, 0), "FL")
    for b in (3, 1):
        for s in S:
            g.pass_on(s, 2, (ALL, b), "R"); g.share(s, (ALL, b, 3))
            g.pass_on(s, 2, (ALL, b), "L"); g.share(s, (ALL, b, 1))
    for s in S:
        g.wait(s, 2, (REST, 0), "FR"); g.wait(s, 2, (REST, 0), "FL")
        g.share(s, (ALL, 0, 2))
    for s in S:
        g.wait(s, 2, (ALL, 2), "R"); g.share(s, (ALL, 2, 3))
        g.wait(s, 2, (ALL, 2), "L"); g.share(s, (ALL, 2, 1))
    for b in (3, 1):
        for s in S:
            g.wait(s, 2, (ALL, b), "FR"); g.wait(s, 2, (ALL, b), "FL")
            g.share(s, (ALL, b, 2))
    for s in S:
        g.wait(s, 2, (ALL, 2), "O"); g.share(s, (ALL, 2, 2))
    for chunk in g.shared:
        g.widen(*chunk)


def kernel(a_ref, b_ref, x_ref, table_ref, o_ref, buf, wide, w_ref, wide_ref, part_ref, mixed_ref, prod_ref, made_ref, w_sem, ss, rs, out_ss, out_rs):
    g = Gather(buf, wide.reshape(2, 4, 4, 4, 16, 2, 8, 128), ss, rs)
    g.knock()
    fetch = pltpu.make_async_copy(table_ref, w_ref, w_sem)
    fetch.start()
    wide_ref[...] = x_ref[...].astype(jnp.float32)
    g.enter()
    regroup(g, wide_ref, part_ref, mixed_ref)
    run_gather(g)
    fetch.wait()
    grp = lax.axis_index("grp")
    core = grp % 2

    def planes(at):
        return [wide[at, n] for n in range(4)]

    def products(block):
        def body(i, c):
            loaded = []
            for u in range(UNROLL):
                p = block * BLOCK + i * UNROLL + u
                loaded.append((planes(a_ref[p]), planes(b_ref[p])))
            for u in range(UNROLL):
                p = i * UNROLL + u
                (ar0, ar1, ai0, ai1), (br0, br1, bi0, bi1) = loaded[u]
                re = (ar0 * br0 + ai0 * bi0) + (ar1 * br1 + ai1 * bi1)
                im = (ai0 * br0 - ar0 * bi0) + (ai1 * br1 - ar1 * bi1)
                prod_ref[pl.ds(p, 8, stride=STRIDE), :] = re
                prod_ref[pl.ds(p + 8 * STRIDE, 8, stride=STRIDE), :] = im
            return c

        lax.fori_loop(0, BLOCK // UNROLL, body, 0)

    def lagged(w):
        cross = jnp.concatenate([prod_ref[j * STRIDE:j * STRIDE + BLOCK, :] for j in range(16)], axis=1)
        return lax.dot_general(
            w, cross.astype(jnp.bfloat16), (((1,), (1,)), ((), ())), preferred_element_type=jnp.float32
        ).astype(jnp.bfloat16)

    def columns(block, n=1):
        return pl.ds(pl.multiple_of(block * BLOCK, 128), n * BLOCK)

    def whole(ref, k):
        return pltpu.make_async_remote_copy(
            src_ref=ref, dst_ref=ref, send_sem=out_ss.at[k], recv_sem=out_rs.at[k], device_id=g.twin, device_id_type=MESH)

    def all_sent(ref, k):
        whole(ref, k).wait_send()

    def all_here(ref, k):
        whole(ref, k).wait_recv()

    def lags_of(group):
        return pl.ds(pl.multiple_of(group * SHORT, SHORT), SHORT)

    def result(j, k, block, sem):
        return pltpu.make_async_remote_copy(
            src_ref=made_ref.at[j, lags_of(grp ^ k)], dst_ref=o_ref.at[:, columns(block)],
            send_sem=out_ss.at[sem], recv_sem=out_rs.at[sem], device_id=g.group[k], device_id_type=MESH)

    def both(j, c):
        products(j)
        made_ref[j] = lagged(w_ref[...])
        block = grp * BOTH + j
        o_ref[:, columns(block)] = made_ref[j, lags_of(grp), :]
        for k in (2, 3, 1):
            result(j, k, block, k).start()
        return c

    def alone(j, c):
        products(BOTH + j)
        chip = pl.ds(pl.multiple_of(grp // 2 * 128, 128), 128)
        made_ref[BOTH + j, chip, :] = lagged(w_ref[chip, :])
        block = 4 * BOTH + core * ALONE + j
        o_ref[:, columns(block)] = made_ref[BOTH + j, lags_of(grp), :]
        result(BOTH + j, 1, block, 0).start()
        return c

    lax.fori_loop(0, BOTH, both, 0)
    lax.fori_loop(0, ALONE, alone, 0)
    for k in (1, 2, 3):
        all_sent(made_ref.at[pl.ds(0, BOTH), lags_of(grp ^ k)], k)
        all_here(o_ref.at[:, columns((grp ^ k) * BOTH, BOTH)], k)
    all_sent(made_ref.at[pl.ds(BOTH, ALONE), lags_of(grp ^ 1)], 0)
    all_here(o_ref.at[:, columns(4 * BOTH + (1 - core) * ALONE, ALONE)], 0)
    for c in g.sent:
        c.wait_send()
    assert g.n == NSEM, g.n


def stack(a, b, x, table):
    smem, vmem = pl.BlockSpec(memory_space=pltpu.SMEM), pl.BlockSpec(memory_space=pltpu.VMEM)
    return pl.pallas_call(
        kernel,
        out_shape=jax.ShapeDtypeStruct((SHORT, SLOTS), jnp.bfloat16),
        in_specs=[smem, smem, vmem, pl.BlockSpec(memory_space=pl.ANY)],
        out_specs=vmem,
        scratch_shapes=[
            pltpu.VMEM((2, 4, 4, 4, 16, 16, 128), jnp.bfloat16),
            pltpu.VMEM((1024, 4, 8, 128), jnp.float32),
            pltpu.VMEM((LAGS, 2 * FREQS), jnp.bfloat16),
            pltpu.VMEM((4, 32, 256), jnp.float32),
            pltpu.VMEM((4, 4, 8, 256), jnp.float32),
            pltpu.VMEM((256, 128), jnp.float32),
            pltpu.VMEM((16 * STRIDE, 128), jnp.float32),
            pltpu.VMEM((BOTH + ALONE, LAGS, BLOCK), jnp.bfloat16),
            pltpu.SemaphoreType.DMA,
            pltpu.SemaphoreType.DMA((SENDS,)),
            pltpu.SemaphoreType.DMA((NSEM,)),
            pltpu.SemaphoreType.DMA((4,)),
            pltpu.SemaphoreType.DMA((4,)),
        ],
        compiler_params=pltpu.CompilerParams(collective_id=0, has_side_effects=True, vmem_limit_bytes=VMEM),
    )(a, b, x, table)


def lag_table():
    span = 4 * FREQS
    lag_index = np.arange(LAGS, dtype=np.int32) - LAGS // 2
    freq_index = np.arange(FREQS, dtype=np.int32) + 1
    phase = np.mod(lag_index[:, None] * freq_index[None, :], span)
    angle = phase.astype(np.float32) * np.float32(2.0 * math.pi / span)
    return np.concatenate([np.cos(angle), -np.sin(angle)], axis=1).astype(ml_dtypes.bfloat16)


def place_of(channel):
    (x0, z0, y0), core0 = where()
    xh, z, y = channel >> 9, (channel >> 7) & 3, (channel >> 5) & 3
    xl, core = (channel >> 4) & 1, (channel >> 3) & 1
    rx, rz, ry = (2 * xh + xl - x0) & 3, (z - z0) & 3, (y - y0) & 3
    pos = ((((core ^ core0) * 4 + rx) * 4 + rz) * 4 + ry)
    return pos * 8 + (channel & 7)


def on_device(spectra, pair_channels, pair_counts):
    grp = lax.axis_index("grp")
    shared = lax.dynamic_slice_in_dim(pair_channels, grp * (BOTH * BLOCK), BOTH * BLOCK, axis=1)
    alone = lax.dynamic_slice_in_dim(pair_channels, (4 * BOTH + grp % 2 * ALONE) * BLOCK, ALONE * BLOCK, axis=1)
    rows = place_of(jnp.concatenate([shared, alone], axis=1))
    raw = stack(rows[0], rows[1], spectra.reshape(4, 32, 256), jnp.asarray(lag_table()))
    live = jnp.arange(SLOTS, dtype=jnp.int32)[None, :] < pair_counts[0]
    return jnp.where(live, raw.astype(jnp.float32) * (1.0 / math.sqrt(WINDOWS * FREQS)), 0.0)


def solution(mesh):
    placed = (P(None, None, "chan", "grp"), P(None, "chan"), P("chan"))
    return jax.shard_map(
        on_device, mesh=mesh, in_specs=placed, out_specs=P("grp", "chan"), check_vma=False
    )
```

```python
import functools
import math

import jax
import jax.numpy as jnp
from jax import lax
from jax.experimental import pallas as pl
from jax.experimental.pallas import tpu as pltpu
from jax.sharding import PartitionSpec as P

FREQS = 1024
LAGS = 256
WINDOWS = 2
SLOTS = 16896
NSEM = 126
SENDS = 24
VMEM = 46 << 20
SHORT = LAGS // 4

BLOCK = 384
BOTH = 9
ALONE = 4
assert 4 * BOTH + 2 * ALONE == SLOTS // BLOCK
MINE = (BOTH + ALONE) * BLOCK
UNROLL = 96
STRIDE = BLOCK + 8
BEHIND = 6

AX = {"x": 0, "z": 1, "y": 2}
MESH = pl.DeviceIdType.MESH
STREAMS = [("yzx", 0, 3, 3), ("zxy", 6, 3, 2), ("xyz", 11, 2, 3)]
HALVES = {"R": "all", "L": "all", "O": "all", "FR": "a", "FL": "b"}
LANDS = {"R": 3, "L": 1, "O": 2, "FR": 2, "FL": 2}

def where():
    chan, grp = lax.axis_index("chan"), lax.axis_index("grp")
    return [2 * (chan // 16) + grp // 2, (chan // 4) % 4, chan % 4], grp % 2

def device(pos, core):
    x, z, y = pos
    return ((x // 2) * 16 + z * 4 + y, (x % 2) * 2 + core)

def moved(pos, axis, by):
    new = list(pos); new[AX[axis]] = (pos[AX[axis]] + by + 4) % 4
    return new

class Gather:
    def __init__(self, buf, table, send_sems, recv_sems):
        self.table = table
        self.buf, self.ss, self.rs = buf, send_sems, recv_sems
        self.pos, self.core = where()
        self.twin = device(self.pos, 1 - self.core)
        peer = [self.pos[0] ^ 1, self.pos[1], self.pos[2]]
        self.group = [None, self.twin, device(peer, self.core), device(peer, 1 - self.core)]
        self.n = 0
        self.sent, self.shared, self.ids = [], [], {}
    def knock(self):
        bar = pltpu.get_barrier_semaphore()
        for ax in "xzy":
            for by in (1, 2, -1):
                pl.semaphore_signal(bar, inc=1, device_id=device(moved(self.pos, ax, by), self.core), device_id_type=MESH)
        for to in (self.twin, self.group[3]):
            pl.semaphore_signal(bar, inc=1, device_id=to, device_id_type=MESH)

    def enter(self):
        pl.semaphore_wait(pltpu.get_barrier_semaphore(), 11)
    def view(self, s, sel, part="all", core=0):
        order, r0, ha, hb = STREAMS[s]
        rows = {"all": (r0, ha + hb), "a": (r0, ha), "b": (r0 + ha, hb)}[part]
        ix = [0, 0, 0]
        for ax, v in zip(order, sel):
            ix[AX[ax]] = v
        return self.buf.at[(core, *ix, pl.ds(*rows))]
    def copy(self, src, dst, k, to):
        return pltpu.make_async_remote_copy(src_ref=src, dst_ref=dst, send_sem=self.ss.at[k % SENDS], recv_sem=self.rs.at[k], device_id=to, device_id_type=MESH)
    def go(self, src, dst, to):
        k = self.n; self.n += 1
        if len(self.sent) == SENDS:
            self.sent.pop(0).wait_send()
        c = self.copy(src, dst, k, to); c.start(); self.sent.append(c)
        return k
    def sel(self, phase, chunk, rel):
        return (*chunk[:phase], rel)
    def send(self, s, phase, chunk, kind):
        ax = STREAMS[s][0][phase]
        by = {"R": 1, "FR": 1, "L": -1, "FL": -1, "O": 2}[kind]
        src_rel = {"R": 0, "L": 0, "O": 0, "FR": 3, "FL": 1}[kind]
        part = HALVES[kind]
        k = self.go(self.view(s, (*chunk, src_rel), part), self.view(s, (*chunk, LANDS[kind]), part), device(moved(self.pos, ax, by), self.core))
        self.ids[s, phase, str(chunk), kind] = k
    def both(self, s, phase, chunk):
        self.send(s, phase, chunk, "R"); self.send(s, phase, chunk, "L")
    def three(self, s, phase, chunk):
        self.both(s, phase, chunk); self.send(s, phase, chunk, "O")
    def wait3(self, s, phase, chunk):
        for kind in ("R", "L", "O"):
            self.wait(s, phase, chunk, kind)
    def wait(self, s, phase, chunk, kind):
        ref = self.view(s, (*chunk, LANDS[kind]), HALVES[kind])
        self.copy(ref, ref, self.ids[s, phase, str(chunk), kind], self.twin).wait_recv()
    def pass_on(self, s, phase, chunk, kind):
        self.wait(s, phase, chunk, kind)
        self.send(s, phase, chunk, "F" + kind)
    def share(self, s, sel, part="all"):
        k = self.go(self.view(s, sel, part, 0), self.view(s, sel, part, 1), self.twin)
        self.shared.append((k, s, sel, part))
        if len(self.shared) > BEHIND:
            self.widen(*self.shared.pop(0))

    def widen(self, k, s, sel, part):
        ref = self.view(s, sel, part, 1)
        self.copy(ref, ref, k, self.twin).wait_recv()
        order, u0, ha, hb = STREAMS[s]
        units = {"all": (u0, ha + hb), "a": (u0, ha), "b": (u0 + ha, hb)}[part]
        spans = [(v.start, v.stop - v.start) if isinstance(v, slice) else (v, 1) for v in sel]

        def one(i, c):
            ix = [0, 0, 0]
            for ax, (first, n) in zip(reversed(order), reversed(spans)):
                ix[AX[ax]] = first + i % n
                i = i // n
            for core in (0, 1):
                at = (core, *ix, pl.ds(*units))
                self.table[at] = self.buf[at].astype(jnp.float32).reshape(units[1], 2, 8, 128)
            return c

        lax.fori_loop(0, math.prod(n for _, n in spans), one, 0)


ALL, REST = slice(0, 4), slice(1, 4)

def regroup(g, wide_ref, part_ref, mixed_ref):
    grp = lax.axis_index("grp")

    def rows_for(group):
        return wide_ref.at[:, pl.ds(pl.multiple_of(8 * group, 8), 8), :]

    ks = [g.go(rows_for(grp ^ k), part_ref.at[k], g.group[k]) for k in (1, 2, 3)]
    for k in range(4):
        got = part_ref.at[k] if k else rows_for(grp)
        if k:
            g.copy(got, got, ks[k - 1], g.twin).wait_recv()
        for plane in range(4):
            for r in range(2):
                mixed_ref[pl.ds(8 * plane + 2 * (grp ^ k) + r, 8, stride=32), :] = got[plane, :, r * 128:(r + 1) * 128]
    g.buf[0, 0, 0, 0] = mixed_ref[...].astype(jnp.bfloat16).reshape(16, 16, 128)


def cosine(phase):
    x = (1024 - jnp.minimum(phase, 4096 - phase)).astype(jnp.float32) * (2.0 * math.pi / 4096)
    y = x * x
    total = jnp.float32(-1 / math.factorial(11))
    for n, sign in ((9, 1), (7, -1), (5, 1), (3, -1), (1, 1)):
        total = total * y + sign / math.factorial(n)
    return x * total


def lag_table(w_ref, chunks):
    def chunk(i, c):
        lag = i * 16 - LAGS // 2 + lax.broadcasted_iota(jnp.int32, (16, FREQS), 0)
        k = 1 + lax.broadcasted_iota(jnp.int32, (16, FREQS), 1)
        phase = (lag * k) & 4095
        rows = pl.ds(pl.multiple_of(i * 16, 16), 16)
        w_ref[rows, :FREQS] = cosine(phase).astype(jnp.bfloat16)
        w_ref[rows, FREQS:] = cosine((phase + 1024) & 4095).astype(jnp.bfloat16)
        return c

    lax.fori_loop(*chunks, chunk, 0)


def run_gather(g, w_ref):
    S = range(len(STREAMS))
    for s in S: g.three(s, 0, ())
    for s in S: g.three(s, 1, (0,))
    for s in S: g.both(s, 2, (0, 0))
    lag_table(w_ref, (0, 8))
    for s in S:
        g.wait3(s, 0, ())
        g.three(s, 1, (REST,))
    for s in S:
        g.both(s, 2, (REST, 0))
    lag_table(w_ref, (8, 16))
    for s in S:
        g.pass_on(s, 2, (0, 0), "R"); g.pass_on(s, 2, (0, 0), "L")
    for s in S:
        g.wait3(s, 1, (0,))
    for s in S:
        g.wait(s, 1, (REST,), "R")
        g.both(s, 2, (ALL, 3))
        g.wait(s, 1, (REST,), "L")
        g.both(s, 2, (ALL, 1))
    for s in S:
        g.pass_on(s, 2, (REST, 0), "R"); g.pass_on(s, 2, (REST, 0), "L")
        g.share(s, (ALL, 0, 3)); g.share(s, (ALL, 0, 1))
    for s in S:
        g.wait(s, 1, (REST,), "O")
        g.three(s, 2, (ALL, 2))
        g.share(s, (ALL, ALL, 0))
    for s in S:
        g.wait(s, 2, (0, 0), "FR"); g.wait(s, 2, (0, 0), "FL")
    for b in (3, 1):
        for s in S:
            g.pass_on(s, 2, (ALL, b), "R"); g.share(s, (ALL, b, 3))
            g.pass_on(s, 2, (ALL, b), "L"); g.share(s, (ALL, b, 1))
    for s in S:
        g.wait(s, 2, (REST, 0), "FR"); g.wait(s, 2, (REST, 0), "FL")
        g.share(s, (ALL, 0, 2))
    for s in S:
        g.wait(s, 2, (ALL, 2), "R"); g.share(s, (ALL, 2, 3))
        g.wait(s, 2, (ALL, 2), "L"); g.share(s, (ALL, 2, 1))
    for b in (3, 1):
        for s in S:
            g.wait(s, 2, (ALL, b), "FR"); g.wait(s, 2, (ALL, b), "FL")
            g.share(s, (ALL, b, 2))
    for s in S:
        g.wait(s, 2, (ALL, 2), "O"); g.share(s, (ALL, 2, 2))
    for chunk in g.shared:
        g.widen(*chunk)


def kernel(a_ref, b_ref, count_ref, x_ref, o_ref, buf, wide, w_ref, wide_ref, part_ref, mixed_ref, prod_ref, made_ref, ss, rs, out_ss, out_rs):
    g = Gather(buf, wide.reshape(2, 4, 4, 4, 16, 2, 8, 128), ss, rs)
    g.knock()
    wide_ref[...] = x_ref[...].astype(jnp.float32)
    g.enter()
    regroup(g, wide_ref, part_ref, mixed_ref)
    run_gather(g, w_ref)
    grp = lax.axis_index("grp")
    core = grp % 2

    def planes(at):
        return [wide[at, n] for n in range(4)]

    def products(block):
        def body(i, c):
            loaded = []
            for u in range(UNROLL):
                p = block * BLOCK + i * UNROLL + u
                loaded.append((planes(a_ref[p]), planes(b_ref[p])))
            for u in range(UNROLL):
                p = i * UNROLL + u
                (ar0, ar1, ai0, ai1), (br0, br1, bi0, bi1) = loaded[u]
                re = (ar0 * br0 + ai0 * bi0) + (ar1 * br1 + ai1 * bi1)
                im = (ai0 * br0 - ar0 * bi0) + (ai1 * br1 - ar1 * bi1)
                prod_ref[pl.ds(p, 8, stride=STRIDE), :] = re
                prod_ref[pl.ds(p + 8 * STRIDE, 8, stride=STRIDE), :] = im
            return c

        lax.fori_loop(0, BLOCK // UNROLL, body, 0)

    def lagged(w, block):
        cross = jnp.concatenate([prod_ref[j * STRIDE:j * STRIDE + BLOCK, :] for j in range(16)], axis=1)
        raw = lax.dot_general(
            w, cross.astype(jnp.bfloat16), (((1,), (1,)), ((), ())), preferred_element_type=jnp.float32
        )
        slot = block * BLOCK + lax.broadcasted_iota(jnp.int32, (1, BLOCK), 1)
        scale = jnp.where(slot < count_ref[0], 1.0 / math.sqrt(WINDOWS * FREQS), 0.0)
        return (raw * scale).astype(jnp.bfloat16)

    def columns(block, n=1):
        return pl.ds(pl.multiple_of(block * BLOCK, 128), n * BLOCK)

    def whole(ref, k):
        return pltpu.make_async_remote_copy(
            src_ref=ref, dst_ref=ref, send_sem=out_ss.at[k], recv_sem=out_rs.at[k], device_id=g.twin, device_id_type=MESH)

    def all_sent(ref, k):
        whole(ref, k).wait_send()

    def all_here(ref, k):
        whole(ref, k).wait_recv()

    def lags_of(group):
        return pl.ds(pl.multiple_of(group * SHORT, SHORT), SHORT)

    def result(j, k, block, sem):
        return pltpu.make_async_remote_copy(
            src_ref=made_ref.at[j, lags_of(grp ^ k)], dst_ref=o_ref.at[:, columns(block)],
            send_sem=out_ss.at[sem], recv_sem=out_rs.at[sem], device_id=g.group[k], device_id_type=MESH)

    def both(j, c):
        products(j)
        block = grp * BOTH + j
        made_ref[j] = lagged(w_ref[...], block)
        o_ref[:, columns(block)] = made_ref[j, lags_of(grp), :]
        for k in (2, 3, 1):
            result(j, k, block, k).start()
        return c

    def alone(j, c):
        products(BOTH + j)
        chip = pl.ds(pl.multiple_of(grp // 2 * 128, 128), 128)
        block = 4 * BOTH + core * ALONE + j
        made_ref[BOTH + j, chip, :] = lagged(w_ref[chip, :], block)
        o_ref[:, columns(block)] = made_ref[BOTH + j, lags_of(grp), :]
        result(BOTH + j, 1, block, 0).start()
        return c

    lax.fori_loop(0, BOTH, both, 0)
    lax.fori_loop(0, ALONE, alone, 0)
    for k in (1, 2, 3):
        all_sent(made_ref.at[pl.ds(0, BOTH), lags_of(grp ^ k)], k)
        all_here(o_ref.at[:, columns((grp ^ k) * BOTH, BOTH)], k)
    all_sent(made_ref.at[pl.ds(BOTH, ALONE), lags_of(grp ^ 1)], 0)
    all_here(o_ref.at[:, columns(4 * BOTH + (1 - core) * ALONE, ALONE)], 0)
    for c in g.sent:
        c.wait_send()
    assert g.n == NSEM, g.n


def stack(a, b, counts, x):
    smem, vmem = pl.BlockSpec(memory_space=pltpu.SMEM), pl.BlockSpec(memory_space=pltpu.VMEM)
    return pl.pallas_call(
        kernel,
        out_shape=jax.ShapeDtypeStruct((SHORT, SLOTS), jnp.bfloat16),
        in_specs=[smem, smem, smem, vmem],
        out_specs=vmem,
        scratch_shapes=[
            pltpu.VMEM((2, 4, 4, 4, 16, 16, 128), jnp.bfloat16),
            pltpu.VMEM((1024, 4, 8, 128), jnp.float32),
            pltpu.VMEM((LAGS, 2 * FREQS), jnp.bfloat16),
            pltpu.VMEM((4, 32, 256), jnp.float32),
            pltpu.VMEM((4, 4, 8, 256), jnp.float32),
            pltpu.VMEM((256, 128), jnp.float32),
            pltpu.VMEM((16 * STRIDE, 128), jnp.float32),
            pltpu.VMEM((BOTH + ALONE, LAGS, BLOCK), jnp.bfloat16),
            pltpu.SemaphoreType.DMA((SENDS,)),
            pltpu.SemaphoreType.DMA((NSEM,)),
            pltpu.SemaphoreType.DMA((4,)),
            pltpu.SemaphoreType.DMA((4,)),
        ],
        compiler_params=pltpu.CompilerParams(collective_id=0, has_side_effects=True, vmem_limit_bytes=VMEM),
    )(a, b, counts, x)


def place_of(channel):
    (x0, z0, y0), core0 = where()
    xh, z, y = channel >> 9, (channel >> 7) & 3, (channel >> 5) & 3
    xl, core = (channel >> 4) & 1, (channel >> 3) & 1
    rx, rz, ry = (2 * xh + xl - x0) & 3, (z - z0) & 3, (y - y0) & 3
    pos = ((((core ^ core0) * 4 + rx) * 4 + rz) * 4 + ry)
    return pos * 8 + (channel & 7)


def on_device(spectra, pair_channels, pair_counts):
    grp = lax.axis_index("grp")
    shared = lax.dynamic_slice_in_dim(pair_channels, grp * (BOTH * BLOCK), BOTH * BLOCK, axis=1)
    alone = lax.dynamic_slice_in_dim(pair_channels, (4 * BOTH + grp % 2 * ALONE) * BLOCK, ALONE * BLOCK, axis=1)
    rows = place_of(jnp.concatenate([shared, alone], axis=1))
    raw = stack(rows[0], rows[1], pair_counts, spectra.reshape(4, 32, 256))
    return raw.astype(jnp.float32)


def solution(mesh):
    placed = (P(None, None, "chan", "grp"), P(None, "chan"), P("chan"))
    return jax.shard_map(
        on_device, mesh=mesh, in_specs=placed, out_specs=P("grp", "chan"), check_vma=False
    )
```

```python
import functools
import math

import jax
import jax.numpy as jnp
from jax import lax
from jax.experimental import pallas as pl
from jax.experimental.pallas import tpu as pltpu
from jax.sharding import PartitionSpec as P

FREQS = 1024
LAGS = 256
WINDOWS = 2
SLOTS = 16896
NSEM = 126
SENDS = 24
VMEM = 46 << 20
SHORT = LAGS // 4

BLOCK = 512
ALONE_BLOCK = 768
BOTH = 6
ALONE = 3
assert 4 * BOTH * BLOCK + 2 * ALONE * ALONE_BLOCK == SLOTS
UNROLL = 64
STRIDE = max(BLOCK, ALONE_BLOCK) + 4
BEHIND = 6

AX = {"x": 0, "z": 1, "y": 2}
MESH = pl.DeviceIdType.MESH
STREAMS = [("yzx", 0, 3, 3), ("zxy", 6, 3, 2), ("xyz", 11, 2, 3)]
HALVES = {"R": "all", "L": "all", "O": "all", "FR": "a", "FL": "b"}
LANDS = {"R": 3, "L": 1, "O": 2, "FR": 2, "FL": 2}

def where():
    chan, grp = lax.axis_index("chan"), lax.axis_index("grp")
    return [2 * (chan // 16) + grp // 2, (chan // 4) % 4, chan % 4], grp % 2

def device(pos, core):
    x, z, y = pos
    return ((x // 2) * 16 + z * 4 + y, (x % 2) * 2 + core)

def moved(pos, axis, by):
    new = list(pos); new[AX[axis]] = (pos[AX[axis]] + by + 4) % 4
    return new

class Gather:
    def __init__(self, buf, table, send_sems, recv_sems):
        self.table = table
        self.buf, self.ss, self.rs = buf, send_sems, recv_sems
        self.pos, self.core = where()
        self.twin = device(self.pos, 1 - self.core)
        peer = [self.pos[0] ^ 1, self.pos[1], self.pos[2]]
        self.group = [None, self.twin, device(peer, self.core), device(peer, 1 - self.core)]
        self.n = 0
        self.sent, self.shared, self.ids = [], [], {}
    def knock(self):
        bar = pltpu.get_barrier_semaphore()
        for ax in "xzy":
            for by in (1, 2, -1):
                pl.semaphore_signal(bar, inc=1, device_id=device(moved(self.pos, ax, by), self.core), device_id_type=MESH)
        for to in (self.twin, self.group[3]):
            pl.semaphore_signal(bar, inc=1, device_id=to, device_id_type=MESH)

    def enter(self):
        pl.semaphore_wait(pltpu.get_barrier_semaphore(), 11)
    def view(self, s, sel, part="all", core=0):
        order, r0, ha, hb = STREAMS[s]
        rows = {"all": (r0, ha + hb), "a": (r0, ha), "b": (r0 + ha, hb)}[part]
        ix = [0, 0, 0]
        for ax, v in zip(order, sel):
            ix[AX[ax]] = v
        return self.buf.at[(core, *ix, pl.ds(*rows))]
    def copy(self, src, dst, k, to):
        return pltpu.make_async_remote_copy(src_ref=src, dst_ref=dst, send_sem=self.ss.at[k % SENDS], recv_sem=self.rs.at[k], device_id=to, device_id_type=MESH)
    def go(self, src, dst, to):
        k = self.n; self.n += 1
        if len(self.sent) == SENDS:
            self.sent.pop(0).wait_send()
        c = self.copy(src, dst, k, to); c.start(); self.sent.append(c)
        return k
    def sel(self, phase, chunk, rel):
        return (*chunk[:phase], rel)
    def send(self, s, phase, chunk, kind):
        ax = STREAMS[s][0][phase]
        by = {"R": 1, "FR": 1, "L": -1, "FL": -1, "O": 2}[kind]
        src_rel = {"R": 0, "L": 0, "O": 0, "FR": 3, "FL": 1}[kind]
        part = HALVES[kind]
        k = self.go(self.view(s, (*chunk, src_rel), part), self.view(s, (*chunk, LANDS[kind]), part), device(moved(self.pos, ax, by), self.core))
        self.ids[s, phase, str(chunk), kind] = k
    def both(self, s, phase, chunk):
        self.send(s, phase, chunk, "R"); self.send(s, phase, chunk, "L")
    def three(self, s, phase, chunk):
        self.both(s, phase, chunk); self.send(s, phase, chunk, "O")
    def wait3(self, s, phase, chunk):
        for kind in ("R", "L", "O"):
            self.wait(s, phase, chunk, kind)
    def wait(self, s, phase, chunk, kind):
        ref = self.view(s, (*chunk, LANDS[kind]), HALVES[kind])
        self.copy(ref, ref, self.ids[s, phase, str(chunk), kind], self.twin).wait_recv()
    def pass_on(self, s, phase, chunk, kind):
        self.wait(s, phase, chunk, kind)
        self.send(s, phase, chunk, "F" + kind)
    def share(self, s, sel, part="all"):
        k = self.go(self.view(s, sel, part, 0), self.view(s, sel, part, 1), self.twin)
        self.shared.append((k, s, sel, part))
        if len(self.shared) > BEHIND:
            self.widen(*self.shared.pop(0))

    def widen(self, k, s, sel, part):
        ref = self.view(s, sel, part, 1)
        self.copy(ref, ref, k, self.twin).wait_recv()
        order, u0, ha, hb = STREAMS[s]
        units = {"all": (u0, ha + hb), "a": (u0, ha), "b": (u0 + ha, hb)}[part]
        spans = [(v.start, v.stop - v.start) if isinstance(v, slice) else (v, 1) for v in sel]

        def one(i, c):
            ix = [0, 0, 0]
            for ax, (first, n) in zip(reversed(order), reversed(spans)):
                ix[AX[ax]] = first + i % n
                i = i // n
            for core in (0, 1):
                at = (core, *ix, pl.ds(*units))
                self.table[at] = self.buf[at].astype(jnp.float32).reshape(units[1], 2, 8, 128)
            return c

        lax.fori_loop(0, math.prod(n for _, n in spans), one, 0)


ALL, REST = slice(0, 4), slice(1, 4)

def regroup(g, wide_ref, part_ref, mixed_ref):
    grp = lax.axis_index("grp")

    def rows_for(group):
        return wide_ref.at[:, pl.ds(pl.multiple_of(8 * group, 8), 8), :]

    ks = [g.go(rows_for(grp ^ k), part_ref.at[k], g.group[k]) for k in (1, 2, 3)]
    for k in range(4):
        got = part_ref.at[k] if k else rows_for(grp)
        if k:
            g.copy(got, got, ks[k - 1], g.twin).wait_recv()
        for plane in range(4):
            for r in range(2):
                mixed_ref[pl.ds(8 * plane + 2 * (grp ^ k) + r, 8, stride=32), :] = got[plane, :, r * 128:(r + 1) * 128]
    g.buf[0, 0, 0, 0] = mixed_ref[...].astype(jnp.bfloat16).reshape(16, 16, 128)


def cosine(phase):
    x = (1024 - jnp.minimum(phase, 4096 - phase)).astype(jnp.float32) * (2.0 * math.pi / 4096)
    y = x * x
    total = jnp.float32(-1 / math.factorial(11))
    for n, sign in ((9, 1), (7, -1), (5, 1), (3, -1), (1, 1)):
        total = total * y + sign / math.factorial(n)
    return x * total


def lag_table(w_ref, chunks):
    def chunk(i, c):
        lag = i * 16 - LAGS // 2 + lax.broadcasted_iota(jnp.int32, (16, FREQS), 0)
        k = 1 + lax.broadcasted_iota(jnp.int32, (16, FREQS), 1)
        phase = (lag * k) & 4095
        rows = pl.ds(pl.multiple_of(i * 16, 16), 16)
        w_ref[rows, :FREQS] = cosine(phase).astype(jnp.bfloat16)
        w_ref[rows, FREQS:] = cosine((phase + 1024) & 4095).astype(jnp.bfloat16)
        return c

    lax.fori_loop(*chunks, chunk, 0)


def run_gather(g, w_ref):
    S = range(len(STREAMS))
    for s in S: g.three(s, 0, ())
    for s in S: g.three(s, 1, (0,))
    for s in S: g.both(s, 2, (0, 0))
    lag_table(w_ref, (0, 8))
    for s in S:
        g.wait3(s, 0, ())
        g.three(s, 1, (REST,))
    for s in S:
        g.both(s, 2, (REST, 0))
    lag_table(w_ref, (8, 16))
    for s in S:
        g.pass_on(s, 2, (0, 0), "R"); g.pass_on(s, 2, (0, 0), "L")
    for s in S:
        g.wait3(s, 1, (0,))
    for s in S:
        g.wait(s, 1, (REST,), "R")
        g.both(s, 2, (ALL, 3))
        g.wait(s, 1, (REST,), "L")
        g.both(s, 2, (ALL, 1))
    for s in S:
        g.pass_on(s, 2, (REST, 0), "R"); g.pass_on(s, 2, (REST, 0), "L")
        g.share(s, (ALL, 0, 3)); g.share(s, (ALL, 0, 1))
    for s in S:
        g.wait(s, 1, (REST,), "O")
        g.three(s, 2, (ALL, 2))
        g.share(s, (ALL, ALL, 0))
    for s in S:
        g.wait(s, 2, (0, 0), "FR"); g.wait(s, 2, (0, 0), "FL")
    for b in (3, 1):
        for s in S:
            g.pass_on(s, 2, (ALL, b), "R"); g.share(s, (ALL, b, 3))
            g.pass_on(s, 2, (ALL, b), "L"); g.share(s, (ALL, b, 1))
    for s in S:
        g.wait(s, 2, (REST, 0), "FR"); g.wait(s, 2, (REST, 0), "FL")
        g.share(s, (ALL, 0, 2))
    for s in S:
        g.wait(s, 2, (ALL, 2), "R"); g.share(s, (ALL, 2, 3))
        g.wait(s, 2, (ALL, 2), "L"); g.share(s, (ALL, 2, 1))
    for b in (3, 1):
        for s in S:
            g.wait(s, 2, (ALL, b), "FR"); g.wait(s, 2, (ALL, b), "FL")
            g.share(s, (ALL, b, 2))
    for s in S:
        g.wait(s, 2, (ALL, 2), "O"); g.share(s, (ALL, 2, 2))
    for chunk in g.shared:
        g.widen(*chunk)


def kernel(a_ref, b_ref, count_ref, x_ref, o_ref, buf, wide, w_ref, wide_ref, part_ref, mixed_ref, prod_ref, made_ref, alone_ref, ss, rs, out_ss, out_rs):
    g = Gather(buf, wide.reshape(2, 4, 4, 4, 16, 2, 8, 128), ss, rs)
    g.knock()
    wide_ref[...] = x_ref[...].astype(jnp.float32)
    g.enter()
    regroup(g, wide_ref, part_ref, mixed_ref)
    run_gather(g, w_ref)
    grp = lax.axis_index("grp")
    core = grp % 2

    def planes(at):
        return [wide[at, n] for n in range(4)]

    def products(first, count):
        def body(i, c):
            loaded = []
            for u in range(UNROLL):
                p = first + i * UNROLL + u
                loaded.append((planes(a_ref[p]), planes(b_ref[p])))
            for u in range(UNROLL):
                p = i * UNROLL + u
                (ar0, ar1, ai0, ai1), (br0, br1, bi0, bi1) = loaded[u]
                re = (ar0 * br0 + ai0 * bi0) + (ar1 * br1 + ai1 * bi1)
                im = (ai0 * br0 - ar0 * bi0) + (ai1 * br1 - ar1 * bi1)
                prod_ref[pl.ds(p, 8, stride=STRIDE), :] = re
                prod_ref[pl.ds(p + 8 * STRIDE, 8, stride=STRIDE), :] = im
            return c

        lax.fori_loop(0, count // UNROLL, body, 0)

    def lagged(w, first, count):
        cross = jnp.concatenate([prod_ref[j * STRIDE:j * STRIDE + count, :] for j in range(16)], axis=1)
        raw = lax.dot_general(
            w, cross.astype(jnp.bfloat16), (((1,), (1,)), ((), ())), preferred_element_type=jnp.float32
        )
        slot = first + lax.broadcasted_iota(jnp.int32, (1, count), 1)
        scale = jnp.where(slot < count_ref[0], 1.0 / math.sqrt(WINDOWS * FREQS), 0.0)
        return (raw * scale).astype(jnp.bfloat16)

    def columns(first, count):
        return pl.ds(pl.multiple_of(first, 128), count)

    def whole(ref, k):
        return pltpu.make_async_remote_copy(
            src_ref=ref, dst_ref=ref, send_sem=out_ss.at[k], recv_sem=out_rs.at[k], device_id=g.twin, device_id_type=MESH)

    def all_sent(ref, k):
        whole(ref, k).wait_send()

    def all_here(ref, k):
        whole(ref, k).wait_recv()

    def lags_of(group):
        return pl.ds(pl.multiple_of(group * SHORT, SHORT), SHORT)

    def result(ref, j, k, cols, sem):
        return pltpu.make_async_remote_copy(
            src_ref=ref.at[j, lags_of(grp ^ k)], dst_ref=o_ref.at[:, cols],
            send_sem=out_ss.at[sem], recv_sem=out_rs.at[sem], device_id=g.group[k], device_id_type=MESH)

    def both(j, c):
        first = (grp * BOTH + j) * BLOCK
        products(j * BLOCK, BLOCK)
        made_ref[j] = lagged(w_ref[...], first, BLOCK)
        cols = columns(first, BLOCK)
        o_ref[:, cols] = made_ref[j, lags_of(grp), :]
        for k in (2, 3, 1):
            result(made_ref, j, k, cols, k).start()
        return c

    def alone(j, c):
        first = 4 * BOTH * BLOCK + (core * ALONE + j) * ALONE_BLOCK
        products(BOTH * BLOCK + j * ALONE_BLOCK, ALONE_BLOCK)
        chip = pl.ds(pl.multiple_of(grp // 2 * 128, 128), 128)
        alone_ref[j, chip, :] = lagged(w_ref[chip, :], first, ALONE_BLOCK)
        cols = columns(first, ALONE_BLOCK)
        o_ref[:, cols] = alone_ref[j, lags_of(grp), :]
        result(alone_ref, j, 1, cols, 0).start()
        return c

    lax.fori_loop(0, BOTH, both, 0)
    lax.fori_loop(0, ALONE, alone, 0)
    for k in (1, 2, 3):
        all_sent(made_ref.at[:, lags_of(grp ^ k)], k)
        all_here(o_ref.at[:, columns((grp ^ k) * BOTH * BLOCK, BOTH * BLOCK)], k)
    all_sent(alone_ref.at[:, lags_of(grp ^ 1)], 0)
    all_here(o_ref.at[:, columns(4 * BOTH * BLOCK + (1 - core) * ALONE * ALONE_BLOCK, ALONE * ALONE_BLOCK)], 0)
    for c in g.sent:
        c.wait_send()
    assert g.n == NSEM, g.n


def stack(a, b, counts, x):
    smem, vmem = pl.BlockSpec(memory_space=pltpu.SMEM), pl.BlockSpec(memory_space=pltpu.VMEM)
    return pl.pallas_call(
        kernel,
        out_shape=jax.ShapeDtypeStruct((SHORT, SLOTS), jnp.bfloat16),
        in_specs=[smem, smem, smem, vmem],
        out_specs=vmem,
        scratch_shapes=[
            pltpu.VMEM((2, 4, 4, 4, 16, 16, 128), jnp.bfloat16),
            pltpu.VMEM((1024, 4, 8, 128), jnp.float32),
            pltpu.VMEM((LAGS, 2 * FREQS), jnp.bfloat16),
            pltpu.VMEM((4, 32, 256), jnp.float32),
            pltpu.VMEM((4, 4, 8, 256), jnp.float32),
            pltpu.VMEM((256, 128), jnp.float32),
            pltpu.VMEM((16 * STRIDE, 128), jnp.float32),
            pltpu.VMEM((BOTH, LAGS, BLOCK), jnp.bfloat16),
            pltpu.VMEM((ALONE, LAGS, ALONE_BLOCK), jnp.bfloat16),
            pltpu.SemaphoreType.DMA((SENDS,)),
            pltpu.SemaphoreType.DMA((NSEM,)),
            pltpu.SemaphoreType.DMA((4,)),
            pltpu.SemaphoreType.DMA((4,)),
        ],
        compiler_params=pltpu.CompilerParams(collective_id=0, has_side_effects=True, vmem_limit_bytes=VMEM),
    )(a, b, counts, x)


def place_of(channel):
    (x0, z0, y0), core0 = where()
    xh, z, y = channel >> 9, (channel >> 7) & 3, (channel >> 5) & 3
    xl, core = (channel >> 4) & 1, (channel >> 3) & 1
    rx, rz, ry = (2 * xh + xl - x0) & 3, (z - z0) & 3, (y - y0) & 3
    pos = ((((core ^ core0) * 4 + rx) * 4 + rz) * 4 + ry)
    return pos * 8 + (channel & 7)


def on_device(spectra, pair_channels, pair_counts):
    grp = lax.axis_index("grp")
    shared = lax.dynamic_slice_in_dim(pair_channels, grp * (BOTH * BLOCK), BOTH * BLOCK, axis=1)
    size = ALONE * ALONE_BLOCK
    alone = lax.dynamic_slice_in_dim(pair_channels, 4 * BOTH * BLOCK + grp % 2 * size, size, axis=1)
    rows = place_of(jnp.concatenate([shared, alone], axis=1))
    raw = stack(rows[0], rows[1], pair_counts, spectra.reshape(4, 32, 256))
    return raw.astype(jnp.float32)


def solution(mesh):
    placed = (P(None, None, "chan", "grp"), P(None, "chan"), P("chan"))
    return jax.shard_map(
        on_device, mesh=mesh, in_specs=placed, out_specs=P("grp", "chan"), check_vma=False
    )
```

```python
import functools
import math

import jax
import jax.numpy as jnp
from jax import lax
from jax.experimental import pallas as pl
from jax.experimental.pallas import tpu as pltpu
from jax.sharding import PartitionSpec as P

FREQS = 1024
LAGS = 256
WINDOWS = 2
SLOTS = 16896
NSEM = 129
SENDS = 24
VMEM = 46 << 20
SHORT = LAGS // 4

BLOCK = 512
ALONE_BLOCK = 768
BOTH = 6
ALONE = 3
assert 4 * BOTH * BLOCK + 2 * ALONE * ALONE_BLOCK == SLOTS
UNROLL = 64
STRIDE = max(BLOCK, ALONE_BLOCK) + 4
BEHIND = 9

AX = {"x": 0, "z": 1, "y": 2}
MESH = pl.DeviceIdType.MESH
STREAMS = [("yzx", 0, 3, 3), ("zxy", 6, 3, 2), ("xyz", 11, 2, 3)]
HALVES = {"R": "all", "L": "all", "O": "all", "FR": "a", "FL": "b"}
LANDS = {"R": 3, "L": 1, "O": 2, "FR": 2, "FL": 2}

def where():
    chan, grp = lax.axis_index("chan"), lax.axis_index("grp")
    return [2 * (chan // 16) + grp // 2, (chan // 4) % 4, chan % 4], grp % 2

def device(pos, core):
    x, z, y = pos
    return ((x // 2) * 16 + z * 4 + y, (x % 2) * 2 + core)

def moved(pos, axis, by):
    new = list(pos); new[AX[axis]] = (pos[AX[axis]] + by + 4) % 4
    return new

class Gather:
    def __init__(self, buf, table, send_sems, recv_sems):
        self.table = table
        self.buf, self.ss, self.rs = buf, send_sems, recv_sems
        self.pos, self.core = where()
        self.twin = device(self.pos, 1 - self.core)
        peer = [self.pos[0] ^ 1, self.pos[1], self.pos[2]]
        self.group = [None, self.twin, device(peer, self.core), device(peer, 1 - self.core)]
        self.n = 0
        self.sent, self.shared, self.ids = [], [], {}
    def knock(self):
        bar = pltpu.get_barrier_semaphore()
        for ax in "xzy":
            for by in (1, 2, -1):
                pl.semaphore_signal(bar, inc=1, device_id=device(moved(self.pos, ax, by), self.core), device_id_type=MESH)
        for to in (self.twin, self.group[3]):
            pl.semaphore_signal(bar, inc=1, device_id=to, device_id_type=MESH)

    def enter(self):
        pl.semaphore_wait(pltpu.get_barrier_semaphore(), 11)
    def view(self, s, sel, part="all", core=0):
        order, r0, ha, hb = STREAMS[s]
        rows = {"all": (r0, ha + hb), "a": (r0, ha), "b": (r0 + ha, hb)}[part]
        ix = [0, 0, 0]
        for ax, v in zip(order, sel):
            ix[AX[ax]] = v
        return self.buf.at[(core, *ix, pl.ds(*rows))]
    def copy(self, src, dst, k, to):
        return pltpu.make_async_remote_copy(src_ref=src, dst_ref=dst, send_sem=self.ss.at[k % SENDS], recv_sem=self.rs.at[k], device_id=to, device_id_type=MESH)
    def go(self, src, dst, to):
        k = self.n; self.n += 1
        if len(self.sent) == SENDS:
            self.sent.pop(0).wait_send()
        c = self.copy(src, dst, k, to); c.start(); self.sent.append(c)
        return k
    def sel(self, phase, chunk, rel):
        return (*chunk[:phase], rel)
    def send(self, s, phase, chunk, kind):
        ax = STREAMS[s][0][phase]
        by = {"R": 1, "FR": 1, "L": -1, "FL": -1, "O": 2}[kind]
        src_rel = {"R": 0, "L": 0, "O": 0, "FR": 3, "FL": 1}[kind]
        part = HALVES[kind]
        k = self.go(self.view(s, (*chunk, src_rel), part), self.view(s, (*chunk, LANDS[kind]), part), device(moved(self.pos, ax, by), self.core))
        self.ids[s, phase, str(chunk), kind] = k
    def both(self, s, phase, chunk):
        self.send(s, phase, chunk, "R"); self.send(s, phase, chunk, "L")
    def three(self, s, phase, chunk):
        self.both(s, phase, chunk); self.send(s, phase, chunk, "O")
    def wait3(self, s, phase, chunk):
        for kind in ("R", "L", "O"):
            self.wait(s, phase, chunk, kind)
    def wait(self, s, phase, chunk, kind):
        ref = self.view(s, (*chunk, LANDS[kind]), HALVES[kind])
        self.copy(ref, ref, self.ids[s, phase, str(chunk), kind], self.twin).wait_recv()
    def pass_on(self, s, phase, chunk, kind):
        self.wait(s, phase, chunk, kind)
        self.send(s, phase, chunk, "F" + kind)
    def share(self, s, sel, part="all"):
        k = self.go(self.view(s, sel, part, 0), self.view(s, sel, part, 1), self.twin)
        self.shared.append((k, s, sel, part))
        if len(self.shared) > BEHIND:
            self.widen(*self.shared.pop(0))

    def widen(self, k, s, sel, part):
        ref = self.view(s, sel, part, 1)
        self.copy(ref, ref, k, self.twin).wait_recv()
        order, u0, ha, hb = STREAMS[s]
        units = {"all": (u0, ha + hb), "a": (u0, ha), "b": (u0 + ha, hb)}[part]
        spans = [(v.start, v.stop - v.start) if isinstance(v, slice) else (v, 1) for v in sel]

        def one(i, c):
            ix = [0, 0, 0]
            for ax, (first, n) in zip(reversed(order), reversed(spans)):
                ix[AX[ax]] = first + i % n
                i = i // n
            for core in (0, 1):
                at = (core, *ix, pl.ds(*units))
                self.table[at] = self.buf[at].astype(jnp.float32).reshape(units[1], 2, 8, 128)
            return c

        lax.fori_loop(0, math.prod(n for _, n in spans), one, 0)


ALL, REST = slice(0, 4), slice(1, 4)

def regroup(g, wide_ref, part_ref, mixed_ref):
    grp = lax.axis_index("grp")

    def rows_for(group):
        return wide_ref.at[:, pl.ds(pl.multiple_of(8 * group, 8), 8), :]

    ks = [g.go(rows_for(grp ^ k), part_ref.at[k], g.group[k]) for k in (1, 2, 3)]
    for k in range(4):
        got = part_ref.at[k] if k else rows_for(grp)
        if k:
            g.copy(got, got, ks[k - 1], g.twin).wait_recv()
        for plane in range(4):
            for r in range(2):
                mixed_ref[pl.ds(8 * plane + 2 * (grp ^ k) + r, 8, stride=32), :] = got[plane, :, r * 128:(r + 1) * 128]
    g.buf[0, 0, 0, 0] = mixed_ref[:256, :].astype(jnp.bfloat16).reshape(16, 16, 128)


def cosine(phase):
    x = (1024 - jnp.minimum(phase, 4096 - phase)).astype(jnp.float32) * (2.0 * math.pi / 4096)
    y = x * x
    total = jnp.float32(-1 / math.factorial(11))
    for n, sign in ((9, 1), (7, -1), (5, 1), (3, -1), (1, 1)):
        total = total * y + sign / math.factorial(n)
    return x * total


def lag_table(w_ref, chunks):
    def chunk(i, c):
        lag = i * 16 - LAGS // 2 + lax.broadcasted_iota(jnp.int32, (16, FREQS), 0)
        k = 1 + lax.broadcasted_iota(jnp.int32, (16, FREQS), 1)
        phase = (lag * k) & 4095
        rows = pl.ds(pl.multiple_of(i * 16, 16), 16)
        w_ref[rows, :FREQS] = cosine(phase).astype(jnp.bfloat16)
        w_ref[rows, FREQS:] = cosine((phase + 1024) & 4095).astype(jnp.bfloat16)
        return c

    lax.fori_loop(*chunks, chunk, 0)


def run_gather(g, w_ref):
    S = range(len(STREAMS))
    for s in S: g.three(s, 0, ())
    for s in S: g.three(s, 1, (0,))
    for s in S: g.both(s, 2, (0, 0))
    lag_table(w_ref, (0, 8))
    for s in S:
        g.wait3(s, 0, ())
        g.three(s, 1, (REST,))
    for s in S:
        g.both(s, 2, (REST, 0))
    lag_table(w_ref, (8, 16))
    for s in S:
        g.pass_on(s, 2, (0, 0), "R"); g.pass_on(s, 2, (0, 0), "L")
    for s in S:
        g.wait3(s, 1, (0,))
    for s in S:
        g.wait(s, 1, (REST,), "R")
        g.both(s, 2, (ALL, 3))
        g.wait(s, 1, (REST,), "L")
        g.both(s, 2, (ALL, 1))
    for s in S:
        g.pass_on(s, 2, (REST, 0), "R"); g.pass_on(s, 2, (REST, 0), "L")
        g.share(s, (ALL, 0, 3)); g.share(s, (ALL, 0, 1))
    for s in S:
        g.wait(s, 1, (REST,), "O")
        g.both(s, 2, (ALL, 2))
        g.share(s, (ALL, ALL, 0))
    for s in S:
        g.wait(s, 2, (0, 0), "FR"); g.wait(s, 2, (0, 0), "FL")
    for b in (3, 1):
        for s in S:
            g.pass_on(s, 2, (ALL, b), "R"); g.share(s, (ALL, b, 3))
            g.pass_on(s, 2, (ALL, b), "L"); g.share(s, (ALL, b, 1))
    for s in S:
        g.wait(s, 2, (REST, 0), "FR"); g.wait(s, 2, (REST, 0), "FL")
        g.share(s, (ALL, 0, 2))
    for s in S:
        g.pass_on(s, 2, (ALL, 2), "R"); g.share(s, (ALL, 2, 3))
        g.pass_on(s, 2, (ALL, 2), "L"); g.share(s, (ALL, 2, 1))
    for b in (3, 1):
        for s in S:
            g.wait(s, 2, (ALL, b), "FR"); g.wait(s, 2, (ALL, b), "FL")
            g.share(s, (ALL, b, 2))
    for s in S:
        g.wait(s, 2, (ALL, 2), "FR"); g.wait(s, 2, (ALL, 2), "FL"); g.share(s, (ALL, 2, 2))
    for chunk in g.shared:
        g.widen(*chunk)


def kernel(a_ref, b_ref, count_ref, x_ref, o_ref, buf, wide, w_ref, wide_ref, part_ref, mixed_ref, prod_ref, made_ref, alone_ref, ss, rs, out_ss, out_rs):
    g = Gather(buf, wide.reshape(2, 4, 4, 4, 16, 2, 8, 128), ss, rs)
    g.knock()
    wide_ref[...] = x_ref[...].astype(jnp.float32)
    g.enter()
    regroup(g, wide_ref, part_ref, mixed_ref)
    run_gather(g, w_ref)
    grp = lax.axis_index("grp")
    core = grp % 2

    def planes(at):
        return [wide[at, n] for n in range(4)]

    def products(first, count):
        def body(i, c):
            loaded = []
            for u in range(UNROLL):
                p = first + i * UNROLL + u
                loaded.append((planes(a_ref[p]), planes(b_ref[p])))
            for u in range(UNROLL):
                p = i * UNROLL + u
                (ar0, ar1, ai0, ai1), (br0, br1, bi0, bi1) = loaded[u]
                re = (ar0 * br0 + ai0 * bi0) + (ar1 * br1 + ai1 * bi1)
                im = (ai0 * br0 - ar0 * bi0) + (ai1 * br1 - ar1 * bi1)
                prod_ref[pl.ds(p, 8, stride=STRIDE), :] = re
                prod_ref[pl.ds(p + 8 * STRIDE, 8, stride=STRIDE), :] = im
            return c

        lax.fori_loop(0, count // UNROLL, body, 0)

    def lagged(w, first, count):
        cross = jnp.concatenate([prod_ref[j * STRIDE:j * STRIDE + count, :] for j in range(16)], axis=1)
        raw = lax.dot_general(
            w, cross.astype(jnp.bfloat16), (((1,), (1,)), ((), ())), preferred_element_type=jnp.float32
        )
        slot = first + lax.broadcasted_iota(jnp.int32, (1, count), 1)
        scale = jnp.where(slot < count_ref[0], 1.0 / math.sqrt(WINDOWS * FREQS), 0.0)
        return (raw * scale).astype(jnp.bfloat16)

    def columns(first, count):
        return pl.ds(pl.multiple_of(first, 128), count)

    def whole(ref, k):
        return pltpu.make_async_remote_copy(
            src_ref=ref, dst_ref=ref, send_sem=out_ss.at[k], recv_sem=out_rs.at[k], device_id=g.twin, device_id_type=MESH)

    def all_sent(ref, k):
        whole(ref, k).wait_send()

    def all_here(ref, k):
        whole(ref, k).wait_recv()

    def lags_of(group):
        return pl.ds(pl.multiple_of(group * SHORT, SHORT), SHORT)

    def result(ref, j, k, cols, sem):
        return pltpu.make_async_remote_copy(
            src_ref=ref.at[j, lags_of(grp ^ k)], dst_ref=o_ref.at[:, cols],
            send_sem=out_ss.at[sem], recv_sem=out_rs.at[sem], device_id=g.group[k], device_id_type=MESH)

    def both(j, c):
        first = (grp * BOTH + j) * BLOCK
        products(j * BLOCK, BLOCK)
        made_ref[j] = lagged(w_ref[...], first, BLOCK)
        cols = columns(first, BLOCK)
        o_ref[:, cols] = made_ref[j, lags_of(grp), :]
        for k in (2, 3, 1):
            result(made_ref, j, k, cols, k).start()
        return c

    def alone(j, c):
        first = 4 * BOTH * BLOCK + (core * ALONE + j) * ALONE_BLOCK
        products(BOTH * BLOCK + j * ALONE_BLOCK, ALONE_BLOCK)
        chip = pl.ds(pl.multiple_of(grp // 2 * 128, 128), 128)
        alone_ref[j, chip, :] = lagged(w_ref[chip, :], first, ALONE_BLOCK)
        cols = columns(first, ALONE_BLOCK)
        o_ref[:, cols] = alone_ref[j, lags_of(grp), :]
        result(alone_ref, j, 1, cols, 0).start()
        return c

    lax.fori_loop(0, BOTH, both, 0)
    lax.fori_loop(0, ALONE, alone, 0)
    for k in (1, 2, 3):
        all_sent(made_ref.at[:, lags_of(grp ^ k)], k)
        all_here(o_ref.at[:, columns((grp ^ k) * BOTH * BLOCK, BOTH * BLOCK)], k)
    all_sent(alone_ref.at[:, lags_of(grp ^ 1)], 0)
    all_here(o_ref.at[:, columns(4 * BOTH * BLOCK + (1 - core) * ALONE * ALONE_BLOCK, ALONE * ALONE_BLOCK)], 0)
    for c in g.sent:
        c.wait_send()
    assert g.n == NSEM, g.n


def stack(a, b, counts, x):
    smem, vmem = pl.BlockSpec(memory_space=pltpu.SMEM), pl.BlockSpec(memory_space=pltpu.VMEM)
    return pl.pallas_call(
        kernel,
        out_shape=jax.ShapeDtypeStruct((SHORT, SLOTS), jnp.bfloat16),
        in_specs=[smem, smem, smem, vmem],
        out_specs=vmem,
        scratch_shapes=[
            pltpu.VMEM((2, 4, 4, 4, 16, 16, 128), jnp.bfloat16),
            pltpu.VMEM((1024, 4, 8, 128), jnp.float32),
            pltpu.VMEM((LAGS, 2 * FREQS), jnp.bfloat16),
            pltpu.VMEM((4, 32, 256), jnp.float32),
            pltpu.VMEM((4, 4, 8, 256), jnp.float32),
            pltpu.VMEM((288, 128), jnp.float32),
            pltpu.VMEM((17 * STRIDE, 128), jnp.float32),
            pltpu.VMEM((BOTH, LAGS, BLOCK), jnp.bfloat16),
            pltpu.VMEM((ALONE, LAGS, ALONE_BLOCK), jnp.bfloat16),
            pltpu.SemaphoreType.DMA((SENDS,)),
            pltpu.SemaphoreType.DMA((NSEM,)),
            pltpu.SemaphoreType.DMA((4,)),
            pltpu.SemaphoreType.DMA((4,)),
        ],
        compiler_params=pltpu.CompilerParams(collective_id=0, has_side_effects=True, vmem_limit_bytes=VMEM),
    )(a, b, counts, x)


def place_of(channel):
    (x0, z0, y0), core0 = where()
    xh, z, y = channel >> 9, (channel >> 7) & 3, (channel >> 5) & 3
    xl, core = (channel >> 4) & 1, (channel >> 3) & 1
    rx, rz, ry = (2 * xh + xl - x0) & 3, (z - z0) & 3, (y - y0) & 3
    pos = ((((core ^ core0) * 4 + rx) * 4 + rz) * 4 + ry)
    return pos * 8 + (channel & 7)


def on_device(spectra, pair_channels, pair_counts):
    grp = lax.axis_index("grp")
    shared = lax.dynamic_slice_in_dim(pair_channels, grp * (BOTH * BLOCK), BOTH * BLOCK, axis=1)
    size = ALONE * ALONE_BLOCK
    alone = lax.dynamic_slice_in_dim(pair_channels, 4 * BOTH * BLOCK + grp % 2 * size, size, axis=1)
    rows = place_of(jnp.concatenate([shared, alone], axis=1))
    raw = stack(rows[0], rows[1], pair_counts, spectra.reshape(4, 32, 256))
    return raw.astype(jnp.float32)


def solution(mesh):
    placed = (P(None, None, "chan", "grp"), P(None, "chan"), P("chan"))
    return jax.shard_map(
        on_device, mesh=mesh, in_specs=placed, out_specs=P("grp", "chan"), check_vma=False
    )
```

```python
import functools
import math

import jax
import jax.numpy as jnp
from jax import lax
from jax.experimental import pallas as pl
from jax.experimental.pallas import tpu as pltpu
from jax.sharding import PartitionSpec as P

FREQS = 1024
LAGS = 256
WINDOWS = 2
SLOTS = 16896
NSEM = 102
SENDS = 24
VMEM = 46 << 20
SHORT = LAGS // 4

BLOCK = 512
ALONE_BLOCK = 768
BOTH = 6
ALONE = 3
assert 4 * BOTH * BLOCK + 2 * ALONE * ALONE_BLOCK == SLOTS
UNROLL = 64
STRIDE = max(BLOCK, ALONE_BLOCK) + 4
BEHIND = 9

AX = {"x": 0, "z": 1, "y": 2}
MESH = pl.DeviceIdType.MESH
STREAMS = [("yzx", 0, 3, 3), ("zxy", 6, 3, 2), ("xyz", 11, 2, 3)]
HALVES = {"R": "all", "L": "all", "O": "all", "FR": "a", "FL": "b"}
LANDS = {"R": 3, "L": 1, "O": 2, "FR": 2, "FL": 2}

def where():
    chan, grp = lax.axis_index("chan"), lax.axis_index("grp")
    return [2 * (chan // 16) + grp // 2, (chan // 4) % 4, chan % 4], grp % 2

def device(pos, core):
    x, z, y = pos
    return ((x // 2) * 16 + z * 4 + y, (x % 2) * 2 + core)

def moved(pos, axis, by):
    new = list(pos); new[AX[axis]] = (pos[AX[axis]] + by + 4) % 4
    return new

class Gather:
    def __init__(self, buf, table, send_sems, recv_sems):
        self.table = table
        self.buf, self.ss, self.rs = buf, send_sems, recv_sems
        self.pos, self.core = where()
        self.twin = device(self.pos, 1 - self.core)
        peer = [self.pos[0] ^ 1, self.pos[1], self.pos[2]]
        self.group = [None, self.twin, device(peer, self.core), device(peer, 1 - self.core)]
        self.n = self.slot = 0
        self.sent, self.shared, self.ids = [], [], {}
    def knock(self):
        bar = pltpu.get_barrier_semaphore()
        for ax in "xzy":
            for by in (1, 2, -1):
                pl.semaphore_signal(bar, inc=1, device_id=device(moved(self.pos, ax, by), self.core), device_id_type=MESH)
        for to in (self.twin, self.group[3]):
            pl.semaphore_signal(bar, inc=1, device_id=to, device_id_type=MESH)

    def enter(self):
        pl.semaphore_wait(pltpu.get_barrier_semaphore(), 11)
    def view(self, s, sel, part="all", core=0):
        order, r0, ha, hb = STREAMS[s]
        rows = {"all": (r0, ha + hb), "a": (r0, ha), "b": (r0 + ha, hb)}[part]
        ix = [0, 0, 0]
        for ax, v in zip(order, sel):
            ix[AX[ax]] = v
        return self.buf.at[(core, *ix, pl.ds(*rows))]
    def copy(self, src, dst, k, to, slot=0):
        return pltpu.make_async_remote_copy(src_ref=src, dst_ref=dst, send_sem=self.ss.at[slot], recv_sem=self.rs.at[k], device_id=to, device_id_type=MESH)

    def go(self, src, dst, to, key=None):
        k = self.ids.setdefault(key, self.n) if key else self.n
        self.n += k == self.n
        if len(self.sent) == SENDS:
            self.sent.pop(0).wait_send()
        c = self.copy(src, dst, k, to, self.slot % SENDS)
        self.slot += 1
        c.start()
        self.sent.append(c)
        return k

    def sel(self, phase, chunk, rel):
        return (*chunk[:phase], rel)
    def send(self, s, phase, chunk, kind):
        ax = STREAMS[s][0][phase]
        by = {"R": 1, "FR": 1, "L": -1, "FL": -1, "O": 2}[kind]
        src_rel = {"R": 0, "L": 0, "O": 0, "FR": 3, "FL": 1}[kind]
        part = HALVES[kind]
        dst = self.view(s, (*chunk, LANDS[kind]), part)
        kind = "F" if kind in ("FR", "FL") else "all" if phase < 2 and chunk != (REST,) else kind
        self.go(self.view(s, (*chunk, src_rel), part), dst, device(moved(self.pos, ax, by), self.core), (s, phase, str(chunk), kind))

    def both(self, s, phase, chunk):
        self.send(s, phase, chunk, "R"); self.send(s, phase, chunk, "L")
    def three(self, s, phase, chunk):
        self.both(s, phase, chunk); self.send(s, phase, chunk, "O")
    def arrive(self, ref, *key):
        self.copy(ref, ref, self.ids[key], self.twin).wait_recv()

    def wait3(self, s, phase, chunk):
        self.arrive(self.view(s, (*chunk, REST)), s, phase, str(chunk), "all")

    def halves(self, s, chunk):
        self.arrive(self.view(s, (*chunk, 2)), s, 2, str(chunk), "F")

    def wait(self, s, phase, chunk, kind):
        ref = self.view(s, (*chunk, LANDS[kind]), HALVES[kind])
        self.copy(ref, ref, self.ids[s, phase, str(chunk), kind], self.twin).wait_recv()
    def pass_on(self, s, phase, chunk, kind):
        self.wait(s, phase, chunk, kind)
        self.send(s, phase, chunk, "F" + kind)
    def share(self, s, sel, part="all"):
        k = self.go(self.view(s, sel, part, 0), self.view(s, sel, part, 1), self.twin)
        self.shared.append((k, s, sel, part))
        if len(self.shared) > BEHIND:
            self.widen(*self.shared.pop(0))

    def widen(self, k, s, sel, part):
        ref = self.view(s, sel, part, 1)
        self.copy(ref, ref, k, self.twin).wait_recv()
        order, u0, ha, hb = STREAMS[s]
        units = {"all": (u0, ha + hb), "a": (u0, ha), "b": (u0 + ha, hb)}[part]
        spans = [(v.start, v.stop - v.start) if isinstance(v, slice) else (v, 1) for v in sel]

        def one(i, c):
            ix = [0, 0, 0]
            for ax, (first, n) in zip(reversed(order), reversed(spans)):
                ix[AX[ax]] = first + i % n
                i = i // n
            for core in (0, 1):
                at = (core, *ix, pl.ds(*units))
                self.table[at] = self.buf[at].astype(jnp.float32).reshape(units[1], 2, 8, 128)
            return c

        lax.fori_loop(0, math.prod(n for _, n in spans), one, 0)


ALL, REST = slice(0, 4), slice(1, 4)

def regroup(g, wide_ref, part_ref, mixed_ref):
    grp = lax.axis_index("grp")

    def rows_for(group):
        return wide_ref.at[:, pl.ds(pl.multiple_of(8 * group, 8), 8), :]

    ks = [g.go(rows_for(grp ^ k), part_ref.at[k], g.group[k]) for k in (1, 2, 3)]
    for k in range(4):
        got = part_ref.at[k] if k else rows_for(grp)
        if k:
            g.copy(got, got, ks[k - 1], g.twin).wait_recv()
        for plane in range(4):
            for r in range(2):
                mixed_ref[pl.ds(8 * plane + 2 * (grp ^ k) + r, 8, stride=32), :] = got[plane, :, r * 128:(r + 1) * 128]
    g.buf[0, 0, 0, 0] = mixed_ref[:256, :].astype(jnp.bfloat16).reshape(16, 16, 128)


def cosine(phase):
    x = (1024 - jnp.minimum(phase, 4096 - phase)).astype(jnp.float32) * (2.0 * math.pi / 4096)
    y = x * x
    total = jnp.float32(-1 / math.factorial(11))
    for n, sign in ((9, 1), (7, -1), (5, 1), (3, -1), (1, 1)):
        total = total * y + sign / math.factorial(n)
    return x * total


def lag_table(w_ref, chunks):
    def chunk(i, c):
        lag = i * 16 - LAGS // 2 + lax.broadcasted_iota(jnp.int32, (16, FREQS), 0)
        k = 1 + lax.broadcasted_iota(jnp.int32, (16, FREQS), 1)
        phase = (lag * k) & 4095
        rows = pl.ds(pl.multiple_of(i * 16, 16), 16)
        w_ref[rows, :FREQS] = cosine(phase).astype(jnp.bfloat16)
        w_ref[rows, FREQS:] = cosine((phase + 1024) & 4095).astype(jnp.bfloat16)
        return c

    lax.fori_loop(*chunks, chunk, 0)


def run_gather(g, w_ref):
    S = range(len(STREAMS))
    for s in S: g.three(s, 0, ())
    for s in S: g.three(s, 1, (0,))
    for s in S: g.both(s, 2, (0, 0))
    lag_table(w_ref, (0, 16))
    for s in S:
        g.wait3(s, 0, ())
        g.three(s, 1, (REST,))
    for s in S:
        g.both(s, 2, (REST, 0))
    for s in S:
        g.pass_on(s, 2, (0, 0), "R"); g.pass_on(s, 2, (0, 0), "L")
    for s in S:
        g.wait3(s, 1, (0,))
    for s in S:
        g.wait(s, 1, (REST,), "R")
        g.both(s, 2, (ALL, 3))
        g.wait(s, 1, (REST,), "L")
        g.both(s, 2, (ALL, 1))
    for s in S:
        g.pass_on(s, 2, (REST, 0), "R"); g.pass_on(s, 2, (REST, 0), "L")
        g.share(s, (ALL, 0, 3)); g.share(s, (ALL, 0, 1))
    for s in S:
        g.wait(s, 1, (REST,), "O")
        g.both(s, 2, (ALL, 2))
        g.share(s, (ALL, ALL, 0))
    for s in S:
        g.halves(s, (0, 0))
    for b in (3, 1):
        for s in S:
            g.pass_on(s, 2, (ALL, b), "R"); g.share(s, (ALL, b, 3))
            g.pass_on(s, 2, (ALL, b), "L"); g.share(s, (ALL, b, 1))
    for s in S:
        g.halves(s, (REST, 0))
        g.share(s, (ALL, 0, 2))
    for s in S:
        g.pass_on(s, 2, (ALL, 2), "R"); g.share(s, (ALL, 2, 3))
        g.pass_on(s, 2, (ALL, 2), "L"); g.share(s, (ALL, 2, 1))
    for b in (3, 1):
        for s in S:
            g.halves(s, (ALL, b))
            g.share(s, (ALL, b, 2))
    for s in S:
        g.halves(s, (ALL, 2)); g.share(s, (ALL, 2, 2))
    for chunk in g.shared:
        g.widen(*chunk)


def kernel(a_ref, b_ref, count_ref, x_ref, o_ref, buf, wide, w_ref, wide_ref, part_ref, mixed_ref, prod_ref, made_ref, alone_ref, ss, rs, out_ss, out_rs):
    g = Gather(buf, wide.reshape(2, 4, 4, 4, 16, 2, 8, 128), ss, rs)
    g.knock()
    wide_ref[...] = x_ref[...].astype(jnp.float32)
    g.enter()
    regroup(g, wide_ref, part_ref, mixed_ref)
    run_gather(g, w_ref)
    grp = lax.axis_index("grp")
    core = grp % 2

    def planes(at):
        return [wide[at, n] for n in range(4)]

    def products(first, count):
        def body(i, c):
            loaded = []
            for u in range(UNROLL):
                p = first + i * UNROLL + u
                loaded.append((planes(a_ref[p]), planes(b_ref[p])))
            for u in range(UNROLL):
                p = i * UNROLL + u
                (ar0, ar1, ai0, ai1), (br0, br1, bi0, bi1) = loaded[u]
                re = (ar0 * br0 + ai0 * bi0) + (ar1 * br1 + ai1 * bi1)
                im = (ai0 * br0 - ar0 * bi0) + (ai1 * br1 - ar1 * bi1)
                prod_ref[pl.ds(p, 8, stride=STRIDE), :] = re
                prod_ref[pl.ds(p + 8 * STRIDE, 8, stride=STRIDE), :] = im
            return c

        lax.fori_loop(0, count // UNROLL, body, 0)

    def lagged(w, first, count):
        cross = jnp.concatenate([prod_ref[j * STRIDE:j * STRIDE + count, :] for j in range(16)], axis=1)
        raw = lax.dot_general(
            w, cross.astype(jnp.bfloat16), (((1,), (1,)), ((), ())), preferred_element_type=jnp.float32
        )
        slot = first + lax.broadcasted_iota(jnp.int32, (1, count), 1)
        scale = jnp.where(slot < count_ref[0], 1.0 / math.sqrt(WINDOWS * FREQS), 0.0)
        return (raw * scale).astype(jnp.bfloat16)

    def columns(first, count):
        return pl.ds(pl.multiple_of(first, 128), count)

    def whole(ref, k):
        return pltpu.make_async_remote_copy(
            src_ref=ref, dst_ref=ref, send_sem=out_ss.at[k], recv_sem=out_rs.at[k], device_id=g.twin, device_id_type=MESH)

    def all_sent(ref, k):
        whole(ref, k).wait_send()

    def all_here(ref, k):
        whole(ref, k).wait_recv()

    def lags_of(group):
        return pl.ds(pl.multiple_of(group * SHORT, SHORT), SHORT)

    def result(ref, j, k, cols, sem):
        return pltpu.make_async_remote_copy(
            src_ref=ref.at[j, lags_of(grp ^ k)], dst_ref=o_ref.at[:, cols],
            send_sem=out_ss.at[sem], recv_sem=out_rs.at[sem], device_id=g.group[k], device_id_type=MESH)

    def both(j, c):
        first = (grp * BOTH + j) * BLOCK
        products(j * BLOCK, BLOCK)
        made_ref[j] = lagged(w_ref[...], first, BLOCK)
        cols = columns(first, BLOCK)
        o_ref[:, cols] = made_ref[j, lags_of(grp), :]
        for k in (2, 3, 1):
            result(made_ref, j, k, cols, k).start()
        return c

    def alone(j, c):
        first = 4 * BOTH * BLOCK + (core * ALONE + j) * ALONE_BLOCK
        products(BOTH * BLOCK + j * ALONE_BLOCK, ALONE_BLOCK)
        chip = pl.ds(pl.multiple_of(grp // 2 * 128, 128), 128)
        alone_ref[j, chip, :] = lagged(w_ref[chip, :], first, ALONE_BLOCK)
        cols = columns(first, ALONE_BLOCK)
        o_ref[:, cols] = alone_ref[j, lags_of(grp), :]
        result(alone_ref, j, 1, cols, 0).start()
        return c

    lax.fori_loop(0, BOTH, both, 0)
    lax.fori_loop(0, ALONE, alone, 0)
    for k in (1, 2, 3):
        all_sent(made_ref.at[:, lags_of(grp ^ k)], k)
        all_here(o_ref.at[:, columns((grp ^ k) * BOTH * BLOCK, BOTH * BLOCK)], k)
    all_sent(alone_ref.at[:, lags_of(grp ^ 1)], 0)
    all_here(o_ref.at[:, columns(4 * BOTH * BLOCK + (1 - core) * ALONE * ALONE_BLOCK, ALONE * ALONE_BLOCK)], 0)
    for c in g.sent:
        c.wait_send()
    assert g.n == NSEM, g.n


def stack(a, b, counts, x):
    smem, vmem = pl.BlockSpec(memory_space=pltpu.SMEM), pl.BlockSpec(memory_space=pltpu.VMEM)
    return pl.pallas_call(
        kernel,
        out_shape=jax.ShapeDtypeStruct((SHORT, SLOTS), jnp.bfloat16),
        in_specs=[smem, smem, smem, vmem],
        out_specs=vmem,
        scratch_shapes=[
            pltpu.VMEM((2, 4, 4, 4, 16, 16, 128), jnp.bfloat16),
            pltpu.VMEM((1024, 4, 8, 128), jnp.float32),
            pltpu.VMEM((LAGS, 2 * FREQS), jnp.bfloat16),
            pltpu.VMEM((4, 32, 256), jnp.float32),
            pltpu.VMEM((4, 4, 8, 256), jnp.float32),
            pltpu.VMEM((288, 128), jnp.float32),
            pltpu.VMEM((17 * STRIDE, 128), jnp.float32),
            pltpu.VMEM((BOTH, LAGS, BLOCK), jnp.bfloat16),
            pltpu.VMEM((ALONE, LAGS, ALONE_BLOCK), jnp.bfloat16),
            pltpu.SemaphoreType.DMA((SENDS,)),
            pltpu.SemaphoreType.DMA((NSEM,)),
            pltpu.SemaphoreType.DMA((4,)),
            pltpu.SemaphoreType.DMA((4,)),
        ],
        compiler_params=pltpu.CompilerParams(collective_id=0, has_side_effects=True, vmem_limit_bytes=VMEM),
    )(a, b, counts, x)


def place_of(channel):
    (x0, z0, y0), core0 = where()
    xh, z, y = channel >> 9, (channel >> 7) & 3, (channel >> 5) & 3
    xl, core = (channel >> 4) & 1, (channel >> 3) & 1
    rx, rz, ry = (2 * xh + xl - x0) & 3, (z - z0) & 3, (y - y0) & 3
    pos = ((((core ^ core0) * 4 + rx) * 4 + rz) * 4 + ry)
    return pos * 8 + (channel & 7)


def on_device(spectra, pair_channels, pair_counts):
    grp = lax.axis_index("grp")
    shared = lax.dynamic_slice_in_dim(pair_channels, grp * (BOTH * BLOCK), BOTH * BLOCK, axis=1)
    size = ALONE * ALONE_BLOCK
    alone = lax.dynamic_slice_in_dim(pair_channels, 4 * BOTH * BLOCK + grp % 2 * size, size, axis=1)
    rows = place_of(jnp.concatenate([shared, alone], axis=1))
    raw = stack(rows[0], rows[1], pair_counts, spectra.reshape(4, 32, 256))
    return raw.astype(jnp.float32)


def solution(mesh):
    placed = (P(None, None, "chan", "grp"), P(None, "chan"), P("chan"))
    return jax.shard_map(
        on_device, mesh=mesh, in_specs=placed, out_specs=P("grp", "chan"), check_vma=False
    )
```
